32 devices in a mesh: chan: 8 (over y, x, core), tm: 4 (over z).
Axes of the slice: x: 2, y: 2, z: 4, core: 2. Of those that a mesh axis runs over, the one named last changes fastest.
Arguments:
- signals: bfloat16 [2368, 5120], P('chan', 'tm'), may hold values from -6 to 6
- kernels: bfloat16 [2, 640], replicated, may hold values from -0.25 to 0.25
- chan_map: int32 [2368], replicated, may hold values from 0 to 2367, as said below
- crosstalk: bfloat16 [64, 37, 37], P('chan'), may hold values from -0.5 to 0.5
- starts: int32 [64, 4, 1], P(None, 'tm'), may hold values from 0 to 768
- counts: int32 [64, 4], P(None, 'tm'), may hold values from 0 to 1, as said below
Outputs:
- built: bfloat16 [64, 4, 1, 2, 37, 512], P('chan', 'tm')
The draws below stay inside these ranges and needn't reach their ends.
Inputs may be any that keep to these rules, and one draw needn't show every extreme that they name: `chan_map`: a permutation; the rows c with (c mod (296)) // 37 = b name channels of crystals b * 8 to (b + 1) * 8 - 1 only. `counts`: some entry equals 1.
All inputs are finite; a program needn't handle non-finite values.
Results may differ from the reference program's by a relative error of at most 0.005.
Values may be sent and summed in bfloat16 or wider, within the bound.
A program may use at most 128 MiB of HBM per device.

```python
import jax
import jax.numpy as jnp
from jax import lax

SIG = 37
KLEN = 640
SEGLEN = 512
SAMP_DEV = 1280
SLOTS = 1
PRE = 128
CPO = 8
CRYSTALS = 64
CHANNELS = 2368
SHARDS = 4
SAMPLES = 5120


def draw_chan_map(key, part):
    block_size = CPO * SIG

    def one_owner(owner_index):
        return owner_index * block_size + jax.random.permutation(jax.random.fold_in(key, owner_index + 7), block_size)
    table = jax.vmap(one_owner)(jnp.arange(CPO))
    return table.reshape(CPO, CPO, SIG).transpose(1, 0, 2).reshape(CHANNELS).astype(jnp.int32)


def draw_counts(key, part):
    first_key, second_key = jax.random.split(jax.random.fold_in(key, 11))
    base_counts = jax.random.randint(first_key, (CRYSTALS, SHARDS), 0, SLOTS + 1)
    pick_index = jax.random.randint(second_key, (), 0, CRYSTALS * SHARDS)
    flat_index = jnp.arange(CRYSTALS * SHARDS).reshape(CRYSTALS, SHARDS)
    return jnp.where(flat_index == pick_index, SLOTS, base_counts).astype(jnp.int32)


def set_ends(drawn, stream_key, least, high):
    dims = drawn.shape
    index_at = [jax.random.randint(jax.random.fold_in(stream_key, axis), (), 0, dims[axis]) for axis in range(len(dims))]
    drawn = drawn.at[tuple(index_at)].set(least)
    longest = dims.index(max(dims))
    index_at[longest] = (index_at[longest] + 1) % dims[longest]
    return drawn.at[tuple(index_at)].set(high)


def level_of(own_key, dims, cuts, low, largest):
    loudness = 1.0
    for axis_at, blocks in cuts:
        steps = jax.random.uniform(jax.random.fold_in(jax.random.fold_in(own_key, 6), axis_at), (blocks,), jnp.float32, low / len(cuts), largest / len(cuts))
        loudness = loudness * jnp.repeat(jnp.exp(steps), dims[axis_at] // blocks).reshape((-1,) + (1,) * (len(dims) - 1 - axis_at))
    return loudness


def scatter_about(rng, extent, width, bound, cuts=(), kind=jnp.bfloat16):
    array = width * jax.random.normal(rng, extent, jnp.float32)
    if cuts:
        array = array * level_of(rng, extent, cuts, -0.22, 0.18)
    return jnp.clip(array, -bound, bound).astype(kind)


def setup_inputs(seed: int = 0) -> dict:
    streams_of = jax.random.split(jax.random.key(seed), 7)
    signals = scatter_about(streams_of[0], (CHANNELS, SAMPLES), 1.0, 6.0, ((0, 8), (1, 4)))
    kernels = scatter_about(streams_of[1], (2, KLEN), KLEN ** -0.5, 0.25)
    chan_map = draw_chan_map(jax.random.fold_in(streams_of[6], 71), 0)
    crosstalk = scatter_about(streams_of[3], (CRYSTALS, SIG, SIG), 0.08, 0.5, ((0, 8),))
    starts = set_ends(jax.random.randint(streams_of[4], (CRYSTALS, SHARDS, SLOTS), 0, SAMP_DEV - SEGLEN + 1), jax.random.fold_in(streams_of[4], 1), 0, SAMP_DEV - SEGLEN).astype(jnp.int32)
    counts = draw_counts(jax.random.fold_in(streams_of[6], 71), 0)
    return {"signals": signals, "kernels": kernels, "chan_map": chan_map, "crosstalk": crosstalk, "starts": starts, "counts": counts}


def reference(signals, kernels, chan_map, crosstalk, starts, counts):
    length = 1 << (SAMPLES + KLEN - 1).bit_length()
    taps = jnp.fft.rfft(kernels.astype(jnp.float32), n=length, axis=-1)

    def filter_block(block):
        spectra = jnp.fft.rfft(block.astype(jnp.float32), n=length, axis=-1)
        traces = jnp.fft.irfft(spectra[:, None, :] * taps[None], n=length, axis=-1)[:, :, :SAMPLES]
        return traces.astype(jnp.bfloat16)

    filtered = lax.map(filter_block, signals.reshape(CPO, CPO * SIG, SAMPLES)).reshape(CHANNELS, 2, SAMPLES)
    row_of = jnp.argsort(chan_map).astype(jnp.int32)
    center = (PRE - 1) / 2.0
    fit_axis = (jnp.arange(SEGLEN, dtype=jnp.float32) - center) / (PRE / 2.0)
    pre_axis = fit_axis[:PRE]
    shard_grid = jnp.broadcast_to(jnp.arange(SHARDS, dtype=jnp.int32)[:, None], (SHARDS, SLOTS))
    slot_grid = jnp.broadcast_to(jnp.arange(SLOTS, dtype=jnp.int32)[None, :], (SHARDS, SLOTS))

    def build(crystal):
        picks = (crystal * SIG + jnp.arange(SIG, dtype=jnp.int32)).astype(jnp.int32)
        chosen = filtered[row_of[picks]]

        def cut(shard_index, begin_at):
            return lax.dynamic_slice_in_dim(chosen, (shard_index * SAMP_DEV + begin_at).astype(jnp.int32), SEGLEN, 2)

        pieces = jax.vmap(jax.vmap(cut))(shard_grid, starts[crystal].astype(jnp.int32))
        pieces = jnp.transpose(pieces.astype(jnp.float32), (0, 1, 3, 2, 4))
        coupled = pieces + jnp.einsum("st,hjftp->hjfsp", crosstalk[crystal].astype(jnp.float32), pieces)
        offset_fit = jnp.mean(coupled[..., :PRE], axis=-1, keepdims=True)
        slope_fit = jnp.sum(coupled[..., :PRE] * pre_axis, axis=-1, keepdims=True) / jnp.sum(pre_axis * pre_axis)
        fitted = coupled - offset_fit - slope_fit * fit_axis
        live_slot = slot_grid < counts[crystal][:, None]
        return jnp.where(live_slot[:, :, None, None, None], fitted, jnp.zeros_like(fitted)).astype(jnp.bfloat16)

    return lax.map(build, jnp.arange(CRYSTALS, dtype=jnp.int32))
```

```python
import functools

import jax
import jax.numpy as jnp
from jax import lax
from jax.experimental import pallas as pl
from jax.experimental.pallas import tpu as pltpu
from jax.sharding import PartitionSpec as P

SEGLEN = 512
PRE = 128
LANES = 128
TILE = 16
GROUP = 256
SLOT_ROWS = 8
MESH = pl.DeviceIdType.MESH


def round_up(value, step):
    return -(-value // step) * step


def iota(shape, axis):
    return lax.broadcasted_iota(jnp.int32, shape, axis)


def kernel(
    owners, shards, x_ref, taps_ref, map_ref, cross_ref, starts_ref, counts_ref, out_ref,
    pack, arrived, placer, ordered, window, segment, table,
    chan_send, chan_recv, tail_send, tail_recv,
):
    me = lax.axis_index("chan")
    shard = lax.axis_index("tm")
    rows, samples = x_ref.shape
    klen = taps_ref.shape[1]
    crystals, sig = cross_ref.shape[0], cross_ref.shape[1]
    main = 2 * TILE
    rest = sig - main
    groups = TILE // rest
    slot = round_up(sig, SLOT_ROWS)
    height = crystals * slot
    blocks = (samples + klen) // LANES
    half_blocks = klen // LANES
    later = shard < shards - 1

    barrier = pltpu.get_barrier_semaphore()
    for step in range(1, owners):
        pl.semaphore_signal(
            barrier, inc=1, device_id={"chan": lax.rem(me + step, owners)}, device_id_type=MESH
        )

    @pl.when(shard > 0)
    def _():
        pl.semaphore_signal(barrier, inc=1, device_id={"tm": shard - 1}, device_id_type=MESH)

    def rest_row(index):
        turned = index - main
        for group in range(1, groups):
            turned = turned - jnp.where(index >= main + group * rest, rest, 0)
        return jnp.where(index < main, index, main + turned)

    for owner in range(owners):
        base = owner * sig
        low = base // TILE * TILE
        high = min(round_up(base + sig, TILE), rows)
        shape = (main + TILE, high - low)
        index = iota(shape, 0)
        wanted = base + rest_row(index)
        hit = jnp.logical_and(iota(shape, 1) + low == wanted, index < main + groups * rest)
        picker = jnp.where(hit, 1.0, 0.0).astype(jnp.bfloat16)
        picked = jnp.dot(picker, x_ref[low:high, :], preferred_element_type=jnp.float32)
        for half in range(2):
            part = picked[:, half * klen : (half + 1) * klen].astype(jnp.bfloat16)
            pack[half, owner, :, 0:klen] = part[0:TILE]
            pack[half, owner, :, klen : 2 * klen] = part[TILE:main]
            left = picked[main:, half * klen : (half + 1) * klen]
            last = left[:, 2 * GROUP : klen]
            row = iota((TILE, GROUP), 0)
            kept = jnp.where(
                row < rest,
                left[:, 0:GROUP],
                jnp.where(row < 2 * rest, left[:, GROUP : 2 * GROUP], jnp.concatenate([last, last], axis=1)),
            )
            pack[half, owner, :, 2 * klen : 2 * klen + GROUP] = kept.astype(jnp.bfloat16)

    arrived[1, me] = pack[0, me]
    arrived[2, me] = pack[1, me]

    @pl.when(shard == 0)
    def _():
        arrived[0] = jnp.zeros(arrived.shape[1:], arrived.dtype)

    pl.semaphore_wait(barrier, owners - 1 + jnp.where(later, 1, 0))

    def to_owner(half, step):
        peer = lax.rem(me + step, owners)
        return pltpu.make_async_remote_copy(
            src_ref=pack.at[half, peer],
            dst_ref=arrived.at[half + 1, me],
            send_sem=chan_send.at[half, step],
            recv_sem=chan_recv.at[half, step],
            device_id={"chan": peer},
            device_id_type=MESH,
        )

    def from_owner(half, step):
        peer = lax.rem(me + owners - step, owners)
        return pltpu.make_async_remote_copy(
            src_ref=pack.at[half, peer],
            dst_ref=arrived.at[half + 1, peer],
            send_sem=chan_send.at[half, step],
            recv_sem=chan_recv.at[half, step],
            device_id={"chan": peer},
            device_id_type=MESH,
        )

    def onward(step):
        peer = lax.rem(me + owners - step, owners)
        return pltpu.make_async_remote_copy(
            src_ref=arrived.at[2, peer],
            dst_ref=arrived.at[0, peer],
            send_sem=tail_send.at[step],
            recv_sem=tail_recv.at[step],
            device_id={"tm": jnp.minimum(shard + 1, shards - 1)},
            device_id_type=MESH,
        )

    for step in range(1, owners):
        to_owner(1, step).start()

    @pl.when(later)
    def _():
        onward(0).start()

    for step in range(1, owners):
        to_owner(0, step).start()

    taps = taps_ref[...].astype(jnp.float32)
    square = (LANES, LANES)
    upper = iota(square, 1) >= iota(square, 0)
    nothing = jnp.zeros(square, jnp.float32)
    for filter_index in range(taps.shape[0]):
        turned = []
        for block in range(half_blocks):
            row = taps[filter_index : filter_index + 1, block * LANES : (block + 1) * LANES]
            turned.append(pltpu.roll(jnp.broadcast_to(row, square), 0, 1, stride=1, stride_axis=0))
        turned.append(nothing)
        for block in range(half_blocks + 1):
            above = turned[half_blocks - block]
            below = turned[half_blocks - 1 - block] if block < half_blocks else nothing
            table[
                block * LANES : (block + 1) * LANES,
                filter_index * LANES : (filter_index + 1) * LANES,
            ] = jnp.where(upper, above, below).astype(table.dtype)

    for step in range(1, owners):
        from_owner(1, step).wait_recv()

        @pl.when(later)
        def _():
            onward(step).start()

    columns = []
    total = map_ref.shape[1]
    for source in range(owners):
        low = source * rows // LANES * LANES
        high = min(round_up((source + 1) * rows, LANES), total)
        shape = (main + TILE, high - low)
        index = iota(shape, 0)
        wanted = source * rows + me * sig + rest_row(index)
        hit = jnp.logical_and(iota(shape, 1) + low == wanted, index < main + groups * rest)
        names = map_ref[:, low:high].astype(jnp.float32) + 1.0
        columns.append(jnp.sum(jnp.where(hit, names, 0.0), axis=1, keepdims=True))
    column = jnp.concatenate(
        [c[0:TILE] for c in columns] + [c[TILE:main] for c in columns] + [c[main:] for c in columns],
        axis=0,
    )
    depth = owners * (main + TILE)
    width = round_up(height, LANES)
    lane = iota((1, width), 1)
    crystal_of = jnp.zeros((1, width), jnp.int32)
    for crystal in range(1, crystals):
        crystal_of = crystal_of + jnp.where(lane >= crystal * slot, 1, 0)
    signal_of = lane - crystal_of * slot
    wanted = jnp.where(signal_of < sig, crystal_of * sig + signal_of + me * rows + 1, -1)
    matched = jnp.where(column == wanted.astype(jnp.float32), 1.0, 0.0)
    turned = jnp.transpose(matched)[0:height]
    lane = iota((height, depth), 1)
    part_of = jnp.where(lane < owners * main, -1, lane & (TILE - 1))
    for group in range(groups):
        own = jnp.logical_and(part_of >= group * rest, part_of < (group + 1) * rest)
        keep = jnp.logical_or(part_of < 0, own)
        placer[group] = jnp.where(keep, turned, 0.0).astype(placer.dtype)

    def place(part, first_block):
        held = arrived[part].reshape(owners * TILE, arrived.shape[3])
        for group in range(groups):
            low = group * GROUP
            high = min(low + GROUP, klen)
            stacked = jnp.concatenate(
                [
                    held[:, low:high],
                    held[:, klen + low : klen + high],
                    held[:, 2 * klen : 2 * klen + high - low],
                ],
                axis=0,
            )
            rows_out = jnp.dot(placer[group], stacked, preferred_element_type=jnp.float32)
            for block in range((high - low) // LANES):
                ordered[first_block + low // LANES + block] = rows_out[
                    :, block * LANES : (block + 1) * LANES
                ]

    place(2, 2 * half_blocks)
    for step in range(1, owners):
        from_owner(0, step).wait_recv()
    place(1, half_blocks)

    @pl.when(shard > 0)
    def _():
        for step in range(owners):
            onward(step).wait_recv()

    place(0, 0)
    ordered[blocks] = jnp.zeros(ordered.shape[1:], ordered.dtype)

    window_blocks = (SEGLEN + klen) // LANES
    lane = iota((slot, LANES), 1)
    for crystal in range(crystals):
        start = starts_ref[me * crystals + crystal]
        first = start >> 7
        shift = start & (LANES - 1)
        back = (LANES - shift) & (LANES - 1)
        at = slice(crystal * slot, (crystal + 1) * slot)
        rolled = [
            pltpu.roll(ordered[first + block, at, :], back, 1) for block in range(window_blocks + 1)
        ]
        for block in range(window_blocks):
            window[block, at, :] = jnp.where(lane < LANES - shift, rolled[block], rolled[block + 1])

    steps_back = half_blocks + 1
    cut = [window[block].astype(jnp.bfloat16) for block in range(window_blocks)]
    taps_table = table[...]
    for block in range(SEGLEN // LANES):
        wide = jnp.concatenate(cut[block : block + steps_back], axis=1)
        filtered = jnp.dot(wide, taps_table, preferred_element_type=jnp.float32)
        for filter_index in range(taps.shape[0]):
            at = filter_index * SEGLEN + block * LANES
            segment[:, at : at + LANES] = filtered[
                :, filter_index * LANES : (filter_index + 1) * LANES
            ]

    center = (PRE - 1) / 2.0
    fit_axis = (iota((1, SEGLEN), 1).astype(jnp.float32) - center) / (PRE / 2.0)
    pre_axis = fit_axis[:, :PRE]
    power = jnp.sum(pre_axis * pre_axis)
    for crystal in range(crystals):
        live = counts_ref[me * crystals + crystal] > 0
        pieces = segment[crystal * slot : crystal * slot + sig, :].astype(jnp.bfloat16)
        coupled = pieces.astype(jnp.float32) + jnp.dot(
            cross_ref[crystal], pieces, preferred_element_type=jnp.float32
        )
        for filter_index in range(taps.shape[0]):
            own = coupled[:, filter_index * SEGLEN : (filter_index + 1) * SEGLEN]
            head = own[:, :PRE]
            offset_fit = jnp.mean(head, axis=1, keepdims=True)
            slope_fit = jnp.sum(head * pre_axis, axis=1, keepdims=True) / power
            fitted = own - offset_fit - slope_fit * fit_axis
            out_ref[crystal, 0, 0, filter_index] = jnp.where(live, fitted, 0.0).astype(out_ref.dtype)

    for step in range(1, owners):
        to_owner(1, step).wait_send()
        to_owner(0, step).wait_send()

    @pl.when(later)
    def _():
        for step in range(owners):
            onward(step).wait_send()


def body(signals, kernels, chan_map, crosstalk, starts, counts):
    owners = lax.axis_size("chan")
    shards = lax.axis_size("tm")
    rows, samples = signals.shape
    filters, klen = kernels.shape
    crystals, sig, _ = crosstalk.shape
    slots = starts.shape[2]
    height = crystals * round_up(sig, SLOT_ROWS)
    packed = 2 * klen + GROUP
    in_vmem = pl.BlockSpec(memory_space=pltpu.VMEM)
    in_smem = pl.BlockSpec(memory_space=pltpu.SMEM)
    return pl.pallas_call(
        functools.partial(kernel, owners, shards),
        out_shape=jax.ShapeDtypeStruct((crystals, 1, slots, filters, sig, SEGLEN), jnp.bfloat16),
        in_specs=[in_vmem] * 4 + [in_smem] * 2,
        out_specs=in_vmem,
        scratch_shapes=[
            pltpu.VMEM((2, owners, TILE, packed), jnp.bfloat16),
            pltpu.VMEM((3, owners, TILE, packed), jnp.bfloat16),
            pltpu.VMEM((TILE // (sig - 2 * TILE), height, owners * 3 * TILE), jnp.bfloat16),
            pltpu.VMEM(((samples + klen) // LANES + 1, height, LANES), jnp.float32),
            pltpu.VMEM(((SEGLEN + klen) // LANES, height, LANES), jnp.float32),
            pltpu.VMEM((height, filters * SEGLEN), jnp.float32),
            pltpu.VMEM((klen + LANES, filters * LANES), jnp.bfloat16),
            pltpu.SemaphoreType.DMA((2, owners)),
            pltpu.SemaphoreType.DMA((2, owners)),
            pltpu.SemaphoreType.DMA((owners,)),
            pltpu.SemaphoreType.DMA((owners,)),
        ],
        compiler_params=pltpu.CompilerParams(
            collective_id=0, has_side_effects=True, vmem_limit_bytes=40 * 1024 * 1024
        ),
        name="build_events",
    )(signals, kernels, chan_map.reshape(1, -1), crosstalk, starts.reshape(-1), counts.reshape(-1))


def solution(mesh):
    return jax.shard_map(
        body,
        mesh=mesh,
        in_specs=(
            P("chan", "tm"),
            P(),
            P(),
            P("chan", None, None),
            P(None, "tm", None),
            P(None, "tm"),
        ),
        out_specs=P("chan", "tm", None, None, None, None),
        check_vma=False,
    )
```

```python
import functools

import jax
import jax.numpy as jnp
from jax import lax
from jax.experimental import pallas as pl
from jax.experimental.pallas import tpu as pltpu
from jax.sharding import PartitionSpec as P

SEGLEN = 512
PRE = 128
LANES = 128
TILE = 16
GROUP = 256
SLOT_ROWS = 8
MESH = pl.DeviceIdType.MESH


def round_up(value, step):
    return -(-value // step) * step


def iota(shape, axis):
    return lax.broadcasted_iota(jnp.int32, shape, axis)


def kernel(
    owners, shards, x_ref, taps_hbm, map_hbm, cross_hbm, starts_ref, counts_ref, out_ref,
    held, taps_ref, map_ref, cross_ref, pack, arrived, placer, ordered, cross, table,
    load_sem, small_sem, chan_send, chan_recv, tail_send, tail_recv,
):
    me = lax.axis_index("chan")
    shard = lax.axis_index("tm")
    rows, samples = x_ref.shape
    klen = taps_ref.shape[1]
    sig, crystals = cross_ref.shape[0], cross_ref.shape[1]
    main = 2 * TILE
    rest = sig - main
    groups = TILE // rest
    slot = round_up(sig, SLOT_ROWS)
    height = crystals * slot
    blocks = (samples + klen) // LANES
    half_blocks = klen // LANES
    later = shard < shards - 1

    def load(half):
        return pltpu.make_async_copy(
            x_ref.at[:, half * klen : (half + 1) * klen], held.at[half], load_sem.at[half]
        )

    small = [
        pltpu.make_async_copy(source, target, small_sem.at[at])
        for at, (source, target) in enumerate(
            [(taps_hbm, taps_ref), (map_hbm, map_ref), (cross_hbm, cross_ref)]
        )
    ]
    load(1).start()
    load(0).start()
    for copy in small:
        copy.start()

    barrier = pltpu.get_barrier_semaphore()
    for step in range(1, owners):
        pl.semaphore_signal(
            barrier, inc=1, device_id={"chan": lax.rem(me + step, owners)}, device_id_type=MESH
        )

    @pl.when(shard > 0)
    def _():
        pl.semaphore_signal(barrier, inc=1, device_id={"tm": shard - 1}, device_id_type=MESH)

    def rest_row(index):
        turned = index - main
        for group in range(1, groups):
            turned = turned - jnp.where(index >= main + group * rest, rest, 0)
        return jnp.where(index < main, index, main + turned)

    def pack_half(half):
        load(half).wait()
        for owner in range(owners):
            base = owner * sig
            low = base // TILE * TILE
            high = min(round_up(base + sig, TILE), rows)
            shape = (main + TILE, high - low)
            index = iota(shape, 0)
            wanted = base + rest_row(index)
            hit = jnp.logical_and(iota(shape, 1) + low == wanted, index < main + groups * rest)
            picker = jnp.where(hit, 1.0, 0.0).astype(jnp.bfloat16)
            picked = jnp.dot(picker, held[half, low:high, :], preferred_element_type=jnp.float32)
            pack[half, owner, :, 0:klen] = picked[0:TILE].astype(jnp.bfloat16)
            pack[half, owner, :, klen : 2 * klen] = picked[TILE:main].astype(jnp.bfloat16)
            left = picked[main:]
            last = left[:, 2 * GROUP : klen]
            row = iota((TILE, GROUP), 0)
            kept = jnp.where(
                row < rest,
                left[:, 0:GROUP],
                jnp.where(row < 2 * rest, left[:, GROUP : 2 * GROUP], jnp.concatenate([last, last], axis=1)),
            )
            pack[half, owner, :, 2 * klen : 2 * klen + GROUP] = kept.astype(jnp.bfloat16)
        arrived[half + 1, me] = pack[half, me]

    pack_half(1)

    @pl.when(shard == 0)
    def _():
        arrived[0] = jnp.zeros(arrived.shape[1:], arrived.dtype)

    pl.semaphore_wait(barrier, owners - 1 + jnp.where(later, 1, 0))

    def to_owner(half, step):
        peer = lax.rem(me + step, owners)
        return pltpu.make_async_remote_copy(
            src_ref=pack.at[half, peer],
            dst_ref=arrived.at[half + 1, me],
            send_sem=chan_send.at[half, step],
            recv_sem=chan_recv.at[half, step],
            device_id={"chan": peer},
            device_id_type=MESH,
        )

    def from_owner(half, step):
        peer = lax.rem(me + owners - step, owners)
        return pltpu.make_async_remote_copy(
            src_ref=pack.at[half, peer],
            dst_ref=arrived.at[half + 1, peer],
            send_sem=chan_send.at[half, step],
            recv_sem=chan_recv.at[half, step],
            device_id={"chan": peer},
            device_id_type=MESH,
        )

    def onward(step):
        peer = lax.rem(me + owners - step, owners)
        return pltpu.make_async_remote_copy(
            src_ref=arrived.at[2, peer],
            dst_ref=arrived.at[0, peer],
            send_sem=tail_send.at[step],
            recv_sem=tail_recv.at[step],
            device_id={"tm": jnp.minimum(shard + 1, shards - 1)},
            device_id_type=MESH,
        )

    for step in range(1, owners):
        to_owner(1, step).start()

    @pl.when(later)
    def _():
        onward(0).start()

    pack_half(0)
    for step in range(1, owners):
        to_owner(0, step).start()

    for copy in small:
        copy.wait()

    taps = taps_ref[...].astype(jnp.float32)
    square = (LANES, LANES)
    upper = iota(square, 1) >= iota(square, 0)
    nothing = jnp.zeros(square, jnp.float32)
    for filter_index in range(taps.shape[0]):
        turned = []
        for block in range(half_blocks):
            row = taps[filter_index : filter_index + 1, block * LANES : (block + 1) * LANES]
            turned.append(pltpu.roll(jnp.broadcast_to(row, square), 0, 1, stride=1, stride_axis=0))
        turned.append(nothing)
        for block in range(half_blocks + 1):
            above = turned[half_blocks - block]
            below = turned[half_blocks - 1 - block] if block < half_blocks else nothing
            table[
                block * LANES : (block + 1) * LANES,
                filter_index * LANES : (filter_index + 1) * LANES,
            ] = jnp.where(upper, above, below).astype(table.dtype)

    for step in range(1, owners):
        from_owner(1, step).wait_recv()

        @pl.when(later)
        def _():
            onward(step).start()

    columns = []
    total = map_ref.shape[0]
    for source in range(owners):
        low = source * rows // LANES * LANES
        high = min(round_up((source + 1) * rows, LANES), total)
        shape = (main + TILE, high - low)
        index = iota(shape, 0)
        wanted = source * rows + me * sig + rest_row(index)
        hit = jnp.logical_and(iota(shape, 1) + low == wanted, index < main + groups * rest)
        names = (map_ref[low:high].astype(jnp.float32) + 1.0).reshape(1, high - low)
        columns.append(jnp.sum(jnp.where(hit, names, 0.0), axis=1, keepdims=True))
    column = jnp.concatenate(
        [c[0:TILE] for c in columns] + [c[TILE:main] for c in columns] + [c[main:] for c in columns],
        axis=0,
    )
    depth = owners * (main + TILE)
    width = round_up(height, LANES)
    lane = iota((1, width), 1)
    crystal_of = jnp.zeros((1, width), jnp.int32)
    for crystal in range(1, crystals):
        crystal_of = crystal_of + jnp.where(lane >= crystal * slot, 1, 0)
    signal_of = lane - crystal_of * slot
    wanted = jnp.where(signal_of < sig, crystal_of * sig + signal_of + me * rows + 1, -1)
    matched = jnp.where(column == wanted.astype(jnp.float32), 1.0, 0.0)
    turned = jnp.transpose(matched)[0:height]
    cross[...] = jnp.zeros(cross.shape, cross.dtype)
    cross[0 : sig * crystals, 0:sig] = cross_ref[...].astype(jnp.float32).reshape(sig * crystals, sig)
    mixed = []
    for crystal in range(crystals):
        own = cross[pl.ds(crystal, slot, stride=crystals), :][:, 0:slot].astype(jnp.bfloat16)
        rows_in = turned[crystal * slot : (crystal + 1) * slot].astype(jnp.bfloat16)
        mixed.append(jnp.dot(own, rows_in, preferred_element_type=jnp.float32))
    mixed = jnp.concatenate(mixed, axis=0)
    lane = iota((height, depth), 1)
    part_of = jnp.where(lane < owners * main, -1, lane & (TILE - 1))
    for group in range(groups):
        own = jnp.logical_and(part_of >= group * rest, part_of < (group + 1) * rest)
        keep = jnp.logical_or(part_of < 0, own)
        placer[group, :, 0:depth] = jnp.where(keep, turned, 0.0).astype(placer.dtype)
        placer[group, :, depth : 2 * depth] = jnp.where(keep, mixed, 0.0).astype(placer.dtype)

    def place(part, first_block):
        source = arrived[part].reshape(owners * TILE, arrived.shape[3])
        for group in range(groups):
            low = group * GROUP
            high = min(low + GROUP, klen)
            stacked = jnp.concatenate(
                [
                    source[:, low:high],
                    source[:, klen + low : klen + high],
                    source[:, 2 * klen : 2 * klen + high - low],
                ]
                * 2,
                axis=0,
            )
            rows_out = jnp.dot(placer[group], stacked, preferred_element_type=jnp.float32)
            for block in range((high - low) // LANES):
                ordered[first_block + low // LANES + block] = rows_out[
                    :, block * LANES : (block + 1) * LANES
                ]

    place(2, 2 * half_blocks)
    for step in range(1, owners):
        from_owner(0, step).wait_recv()
    place(1, half_blocks)

    @pl.when(shard > 0)
    def _():
        for step in range(owners):
            onward(step).wait_recv()

    place(0, 0)
    ordered[blocks] = jnp.zeros(ordered.shape[1:], ordered.dtype)

    window_blocks = (SEGLEN + klen) // LANES
    seg_blocks = SEGLEN // LANES
    steps_back = half_blocks + 1
    lane = iota((slot, LANES), 1)
    center = (PRE - 1) / 2.0
    fit_axis = [
        (iota((1, LANES), 1).astype(jnp.float32) + (block * LANES - center)) / (PRE / 2.0)
        for block in range(seg_blocks)
    ]
    pre_axis = fit_axis[0]
    power = jnp.sum(pre_axis * pre_axis)
    taps_table = table[...]
    pair = 2 if crystals % 2 == 0 else 1
    high = pair * slot
    for crystal in range(0, crystals, pair):
        windows = []
        for member in range(crystal, crystal + pair):
            start = starts_ref[me * crystals + member]
            first = start >> 7
            shift = start & (LANES - 1)
            back = (LANES - shift) & (LANES - 1)
            at = slice(member * slot, (member + 1) * slot)
            rolled = [
                pltpu.roll(ordered[first + block, at, :], back, 1)
                for block in range(window_blocks + 1)
            ]
            windows.append(
                [
                    jnp.where(lane < LANES - shift, rolled[block], rolled[block + 1])
                    for block in range(window_blocks)
                ]
            )
        cut = [
            jnp.concatenate([w[block] for w in windows], axis=0).astype(jnp.bfloat16)
            for block in range(window_blocks)
        ]
        wide = jnp.concatenate(
            [jnp.concatenate(cut[b : b + steps_back], axis=1) for b in range(seg_blocks)], axis=0
        )
        coupled = jnp.dot(wide, taps_table, preferred_element_type=jnp.float32)
        for filter_index in range(taps.shape[0]):
            own = [
                coupled[b * high : (b + 1) * high, filter_index * LANES : (filter_index + 1) * LANES]
                for b in range(seg_blocks)
            ]
            offset_fit = jnp.mean(own[0], axis=1, keepdims=True)
            slope_fit = jnp.sum(own[0] * pre_axis, axis=1, keepdims=True) / power
            for b in range(seg_blocks):
                fitted = own[b] - offset_fit - slope_fit * fit_axis[b]
                for member in range(pair):
                    live = counts_ref[me * crystals + crystal + member] > 0
                    kept = fitted[member * slot : member * slot + sig]
                    out_ref[
                        crystal + member, 0, 0, filter_index, :, b * LANES : (b + 1) * LANES
                    ] = jnp.where(live, kept, 0.0).astype(out_ref.dtype)

    for step in range(1, owners):
        to_owner(1, step).wait_send()
        to_owner(0, step).wait_send()

    @pl.when(later)
    def _():
        for step in range(owners):
            onward(step).wait_send()


def body(signals, kernels, chan_map, crosstalk, starts, counts):
    owners = lax.axis_size("chan")
    shards = lax.axis_size("tm")
    rows, samples = signals.shape
    filters, klen = kernels.shape
    crystals, sig, _ = crosstalk.shape
    slots = starts.shape[2]
    height = crystals * round_up(sig, SLOT_ROWS)
    packed = 2 * klen + GROUP
    in_vmem = pl.BlockSpec(memory_space=pltpu.VMEM)
    in_smem = pl.BlockSpec(memory_space=pltpu.SMEM)
    in_hbm = pl.BlockSpec(memory_space=pltpu.HBM)
    return pl.pallas_call(
        functools.partial(kernel, owners, shards),
        out_shape=jax.ShapeDtypeStruct((crystals, 1, slots, filters, sig, SEGLEN), jnp.bfloat16),
        in_specs=[in_hbm] * 4 + [in_smem] * 2,
        out_specs=in_vmem,
        scratch_shapes=[
            pltpu.VMEM((2, rows, klen), jnp.bfloat16),
            pltpu.VMEM(kernels.shape, kernels.dtype),
            pltpu.VMEM(chan_map.shape, chan_map.dtype),
            pltpu.VMEM((sig, crystals, sig), crosstalk.dtype),
            pltpu.VMEM((2, owners, TILE, packed), jnp.bfloat16),
            pltpu.VMEM((3, owners, TILE, packed), jnp.bfloat16),
            pltpu.VMEM((TILE // (sig - 2 * TILE), height, 2 * owners * 3 * TILE), jnp.bfloat16),
            pltpu.VMEM(((samples + klen) // LANES + 1, height, LANES), jnp.float32),
            pltpu.VMEM((height, LANES), jnp.float32),
            pltpu.VMEM((klen + LANES, filters * LANES), jnp.bfloat16),
            pltpu.SemaphoreType.DMA((2,)),
            pltpu.SemaphoreType.DMA((3,)),
            pltpu.SemaphoreType.DMA((2, owners)),
            pltpu.SemaphoreType.DMA((2, owners)),
            pltpu.SemaphoreType.DMA((owners,)),
            pltpu.SemaphoreType.DMA((owners,)),
        ],
        compiler_params=pltpu.CompilerParams(
            collective_id=0, has_side_effects=True, vmem_limit_bytes=62 * 1024 * 1024
        ),
        name="build_events",
    )(signals, kernels, chan_map, jnp.transpose(crosstalk, (1, 0, 2)), starts.reshape(-1), counts.reshape(-1))


def solution(mesh):
    return jax.shard_map(
        body,
        mesh=mesh,
        in_specs=(
            P("chan", "tm"),
            P(),
            P(),
            P("chan", None, None),
            P(None, "tm", None),
            P(None, "tm"),
        ),
        out_specs=P("chan", "tm", None, None, None, None),
        check_vma=False,
    )
```

```python
import functools

import jax
import jax.numpy as jnp
from jax import lax
from jax.experimental import pallas as pl
from jax.experimental.pallas import tpu as pltpu
from jax.sharding import PartitionSpec as P

SEGLEN = 512
PRE = 128
LANES = 128
TILE = 16
GROUP = 256
SLOT_ROWS = 8
MESH = pl.DeviceIdType.MESH


def round_up(value, step):
    return -(-value // step) * step


def iota(shape, axis):
    return lax.broadcasted_iota(jnp.int32, shape, axis)


def gather_kernel(
    owners, shards, x_ref, taps_ref, map_ref, cross_ref, ordered, table, coupling,
    pack, arrived, placer, cross, chan_send, chan_recv, tail_send, tail_recv,
):
    me = lax.axis_index("chan")
    shard = lax.axis_index("tm")
    rows, samples = x_ref.shape
    klen = taps_ref.shape[1]
    sig, crystals = cross_ref.shape[0], cross_ref.shape[1]
    main = 2 * TILE
    rest = sig - main
    groups = TILE // rest
    slot = round_up(sig, SLOT_ROWS)
    height = crystals * slot
    blocks = (samples + klen) // LANES
    half_blocks = klen // LANES
    later = shard < shards - 1

    def partner(step):
        if owners & (owners - 1) == 0:
            return me ^ step, me ^ step
        return lax.rem(me + step, owners), lax.rem(me + owners - step, owners)

    steps = [step for low in range(2) for step in range(low, owners, 2)]
    steps = [1] + [step for step in steps if step > 1] if owners > 1 else []

    barrier = pltpu.get_barrier_semaphore()
    for step in range(1, owners):
        pl.semaphore_signal(
            barrier, inc=1, device_id={"chan": partner(step)[0]}, device_id_type=MESH
        )

    @pl.when(shard > 0)
    def _():
        pl.semaphore_signal(barrier, inc=1, device_id={"tm": shard - 1}, device_id_type=MESH)

    def rest_row(index):
        turned = index - main
        for group in range(1, groups):
            turned = turned - jnp.where(index >= main + group * rest, rest, 0)
        return jnp.where(index < main, index, main + turned)

    def pack_half(half):
        for owner in range(owners):
            base = owner * sig
            low = base // TILE * TILE
            high = min(round_up(base + sig, TILE), rows)
            shape = (main + TILE, high - low)
            index = iota(shape, 0)
            wanted = base + rest_row(index)
            hit = jnp.logical_and(iota(shape, 1) + low == wanted, index < main + groups * rest)
            picker = jnp.where(hit, 1.0, 0.0).astype(jnp.bfloat16)
            picked = jnp.dot(picker, x_ref[low:high, half * klen : (half + 1) * klen], preferred_element_type=jnp.float32)
            pack[half, owner, :, 0:klen] = picked[0:TILE].astype(jnp.bfloat16)
            pack[half, owner, :, klen : 2 * klen] = picked[TILE:main].astype(jnp.bfloat16)
            left = picked[main:]
            last = left[:, 2 * GROUP : klen]
            row = iota((TILE, GROUP), 0)
            kept = jnp.where(
                row < rest,
                left[:, 0:GROUP],
                jnp.where(row < 2 * rest, left[:, GROUP : 2 * GROUP], jnp.concatenate([last, last], axis=1)),
            )
            pack[half, owner, :, 2 * klen : 2 * klen + GROUP] = kept.astype(jnp.bfloat16)
        arrived[half + 1, me] = pack[half, me]

    pack_half(1)

    @pl.when(shard == 0)
    def _():
        arrived[0] = jnp.zeros(arrived.shape[1:], arrived.dtype)

    pl.semaphore_wait(barrier, owners - 1 + jnp.where(later, 1, 0))

    def to_owner(half, step):
        peer = partner(step)[0]
        return pltpu.make_async_remote_copy(
            src_ref=pack.at[half, peer],
            dst_ref=arrived.at[half + 1, me],
            send_sem=chan_send.at[half, step],
            recv_sem=chan_recv.at[half, step],
            device_id={"chan": peer},
            device_id_type=MESH,
        )

    def from_owner(half, step):
        peer = partner(step)[1]
        return pltpu.make_async_remote_copy(
            src_ref=pack.at[half, peer],
            dst_ref=arrived.at[half + 1, peer],
            send_sem=chan_send.at[half, step],
            recv_sem=chan_recv.at[half, step],
            device_id={"chan": peer},
            device_id_type=MESH,
        )

    def onward(step):
        peer = partner(step)[1] if step else me
        return pltpu.make_async_remote_copy(
            src_ref=arrived.at[2, peer],
            dst_ref=arrived.at[0, peer],
            send_sem=tail_send.at[step],
            recv_sem=tail_recv.at[step],
            device_id={"tm": jnp.minimum(shard + 1, shards - 1)},
            device_id_type=MESH,
        )

    for step in steps:
        to_owner(1, step).start()

    @pl.when(later)
    def _():
        onward(0).start()

    pack_half(0)
    for step in steps:
        to_owner(0, step).start()

    taps = taps_ref[...].astype(jnp.float32)
    square = (LANES, LANES)
    upper = iota(square, 1) >= iota(square, 0)
    nothing = jnp.zeros(square, jnp.float32)
    for filter_index in range(taps.shape[0]):
        turned = []
        for block in range(half_blocks):
            row = taps[filter_index : filter_index + 1, block * LANES : (block + 1) * LANES]
            turned.append(pltpu.roll(jnp.broadcast_to(row, square), 0, 1, stride=1, stride_axis=0))
        turned.append(nothing)
        for block in range(half_blocks + 1):
            above = turned[half_blocks - block]
            below = turned[half_blocks - 1 - block] if block < half_blocks else nothing
            table[
                block * LANES : (block + 1) * LANES,
                filter_index * LANES : (filter_index + 1) * LANES,
            ] = jnp.where(upper, above, below).astype(table.dtype)

    for step in steps:
        from_owner(1, step).wait_recv()

        @pl.when(later)
        def _():
            onward(step).start()

    columns = []
    total = map_ref.shape[0]
    for source in range(owners):
        low = source * rows // LANES * LANES
        high = min(round_up((source + 1) * rows, LANES), total)
        shape = (main + TILE, high - low)
        index = iota(shape, 0)
        wanted = source * rows + me * sig + rest_row(index)
        hit = jnp.logical_and(iota(shape, 1) + low == wanted, index < main + groups * rest)
        names = (map_ref[low:high].astype(jnp.float32) + 1.0).reshape(1, high - low)
        columns.append(jnp.sum(jnp.where(hit, names, 0.0), axis=1, keepdims=True))
    column = jnp.concatenate(
        [c[0:TILE] for c in columns] + [c[TILE:main] for c in columns] + [c[main:] for c in columns],
        axis=0,
    )
    depth = owners * (main + TILE)
    width = round_up(height, LANES)
    lane = iota((1, width), 1)
    crystal_of = jnp.zeros((1, width), jnp.int32)
    for crystal in range(1, crystals):
        crystal_of = crystal_of + jnp.where(lane >= crystal * slot, 1, 0)
    signal_of = lane - crystal_of * slot
    wanted = jnp.where(signal_of < sig, crystal_of * sig + signal_of + me * rows + 1, -1)
    matched = jnp.where(column == wanted.astype(jnp.float32), 1.0, 0.0)
    turned = jnp.transpose(matched)[0:height]
    cross[...] = jnp.zeros(cross.shape, cross.dtype)
    cross[0 : sig * crystals, 0:sig] = cross_ref[...].astype(jnp.float32).reshape(sig * crystals, sig)
    for crystal in range(crystals):
        coupling[crystal] = cross[pl.ds(crystal, slot, stride=crystals), :]
    lane = iota((height, depth), 1)
    part_of = jnp.where(lane < owners * main, -1, lane & (TILE - 1))
    for group in range(groups):
        own = jnp.logical_and(part_of >= group * rest, part_of < (group + 1) * rest)
        keep = jnp.logical_or(part_of < 0, own)
        placer[group] = jnp.where(keep, turned, 0.0).astype(placer.dtype)

    def place(part, first_block):
        source = arrived[part].reshape(owners * TILE, arrived.shape[3])
        for group in range(groups):
            low = group * GROUP
            high = min(low + GROUP, klen)
            stacked = jnp.concatenate(
                [
                    source[:, low:high],
                    source[:, klen + low : klen + high],
                    source[:, 2 * klen : 2 * klen + high - low],
                ],
                axis=0,
            )
            rows_out = jnp.dot(placer[group], stacked, preferred_element_type=jnp.float32)
            for block in range((high - low) // LANES):
                ordered[first_block + low // LANES + block] = rows_out[
                    :, block * LANES : (block + 1) * LANES
                ]

    place(2, 2 * half_blocks)
    for step in steps:
        from_owner(0, step).wait_recv()
    place(1, half_blocks)

    @pl.when(shard > 0)
    def _():
        for step in range(owners):
            onward(step).wait_recv()

    place(0, 0)
    ordered[blocks] = jnp.zeros(ordered.shape[1:], ordered.dtype)

    for step in steps:
        to_owner(1, step).wait_send()
        to_owner(0, step).wait_send()

    @pl.when(later)
    def _():
        for step in range(owners):
            onward(step).wait_send()


def build_kernel(
    sig, ordered, table, coupling, starts_ref, counts_ref, out_ref, rows_of, built, out_sem
):
    me = lax.axis_index("chan")
    crystals, slot = coupling.shape[0], coupling.shape[1]
    filters = table.shape[1] // LANES
    half_blocks = table.shape[0] // LANES - 1
    klen = half_blocks * LANES

    window_blocks = (SEGLEN + klen) // LANES
    seg_blocks = SEGLEN // LANES
    steps_back = half_blocks + 1
    lane = iota((slot, LANES), 1)
    center = (PRE - 1) / 2.0
    fit_axis = [
        (iota((1, LANES), 1).astype(jnp.float32) + (block * LANES - center)) / (PRE / 2.0)
        for block in range(seg_blocks)
    ]
    pre_axis = fit_axis[0]
    power = jnp.sum(pre_axis * pre_axis)
    taps_table = table[...]
    pair = 2 if crystals % 2 == 0 else 1
    high = pair * slot
    for crystal in range(0, crystals, pair):
        windows = []
        for member in range(crystal, crystal + pair):
            start = starts_ref[me * crystals + member]
            first = start >> 7
            shift = start & (LANES - 1)
            back = (LANES - shift) & (LANES - 1)
            at = slice(member * slot, (member + 1) * slot)
            rolled = [
                pltpu.roll(ordered[first + block, at, :], back, 1)
                for block in range(window_blocks + 1)
            ]
            windows.append(
                [
                    jnp.where(lane < LANES - shift, rolled[block], rolled[block + 1])
                    for block in range(window_blocks)
                ]
            )
        cut = [
            jnp.concatenate([w[block] for w in windows], axis=0).astype(jnp.bfloat16)
            for block in range(window_blocks)
        ]
        wide = jnp.concatenate(
            [jnp.concatenate(cut[b : b + steps_back], axis=1) for b in range(seg_blocks)], axis=0
        )
        filtered = jnp.dot(wide, taps_table, preferred_element_type=jnp.float32)
        for member in range(pair):
            at = crystal + member
            live = counts_ref[me * crystals + at] > 0
            pieces = jnp.concatenate(
                [
                    filtered[b * high + member * slot : b * high + (member + 1) * slot]
                    for b in range(seg_blocks)
                ],
                axis=1,
            ).astype(jnp.bfloat16)
            mixer = coupling[at][:, 0:slot].astype(jnp.bfloat16)
            coupled = pieces.astype(jnp.float32) + jnp.dot(
                mixer, pieces, preferred_element_type=jnp.float32
            )
            for filter_index in range(filters):
                own = [
                    coupled[:, (b * filters + filter_index) * LANES :][:, :LANES]
                    for b in range(seg_blocks)
                ]
                offset_fit = jnp.mean(own[0], axis=1, keepdims=True)
                slope_fit = jnp.sum(own[0] * pre_axis, axis=1, keepdims=True) / power
                for b in range(seg_blocks):
                    fitted = own[b] - offset_fit - slope_fit * fit_axis[b]
                    rows_of[
                        at, pl.ds(b * filters + filter_index, slot, stride=filters * seg_blocks), :
                    ] = jnp.where(live, fitted, 0.0)
            built[at] = rows_of[at, 0 : built.shape[1], :].astype(built.dtype)
            pltpu.make_async_copy(built.at[at], out_ref.at[at], out_sem.at[at]).start()
    for at in range(crystals):
        pltpu.make_async_copy(built.at[at], out_ref.at[at], out_sem.at[at]).wait()


def body(signals, kernels, chan_map, crosstalk, starts, counts):
    owners = lax.axis_size("chan")
    shards = lax.axis_size("tm")
    rows, samples = signals.shape
    filters, klen = kernels.shape
    crystals, sig, _ = crosstalk.shape
    slots = starts.shape[2]
    slot = round_up(sig, SLOT_ROWS)
    height = crystals * slot
    packed = 2 * klen + GROUP
    blocks = SEGLEN // LANES
    in_vmem = pl.BlockSpec(memory_space=pltpu.VMEM)
    in_smem = pl.BlockSpec(memory_space=pltpu.SMEM)
    in_hbm = pl.BlockSpec(memory_space=pltpu.HBM)
    ordered, table, coupling = pl.pallas_call(
        functools.partial(gather_kernel, owners, shards),
        out_shape=(
            jax.ShapeDtypeStruct(((samples + klen) // LANES + 1, height, LANES), jnp.float32),
            jax.ShapeDtypeStruct((klen + LANES, filters * LANES), jnp.bfloat16),
            jax.ShapeDtypeStruct((crystals, slot, LANES), jnp.float32),
        ),
        in_specs=[in_vmem] * 4,
        out_specs=(in_vmem,) * 3,
        scratch_shapes=[
            pltpu.VMEM((2, owners, TILE, packed), jnp.bfloat16),
            pltpu.VMEM((3, owners, TILE, packed), jnp.bfloat16),
            pltpu.VMEM((TILE // (sig - 2 * TILE), height, owners * 3 * TILE), jnp.bfloat16),
            pltpu.VMEM((height, LANES), jnp.float32),
            pltpu.SemaphoreType.DMA((2, owners)),
            pltpu.SemaphoreType.DMA((2, owners)),
            pltpu.SemaphoreType.DMA((owners,)),
            pltpu.SemaphoreType.DMA((owners,)),
        ],
        compiler_params=pltpu.CompilerParams(
            collective_id=0, has_side_effects=True, vmem_limit_bytes=32 * 1024 * 1024
        ),
        name="gather_rows",
    )(signals, kernels, chan_map, jnp.transpose(crosstalk, (1, 0, 2)))
    built = pl.pallas_call(
        functools.partial(build_kernel, sig),
        out_shape=jax.ShapeDtypeStruct((crystals, sig * blocks * filters, LANES), jnp.bfloat16),
        in_specs=[in_vmem] * 3 + [in_smem] * 2,
        out_specs=in_hbm,
        scratch_shapes=[
            pltpu.VMEM((crystals, slot * blocks * filters, LANES), jnp.float32),
            pltpu.VMEM((crystals, sig * blocks * filters, LANES), jnp.bfloat16),
            pltpu.SemaphoreType.DMA((crystals,)),
        ],
        compiler_params=pltpu.CompilerParams(vmem_limit_bytes=32 * 1024 * 1024),
        name="build_events",
    )(ordered, table, coupling, starts.reshape(-1), counts.reshape(-1))
    parts = built.reshape(crystals, sig, blocks, filters, LANES)
    return jnp.transpose(parts, (0, 3, 1, 2, 4)).reshape(crystals, 1, slots, filters, sig, SEGLEN)


def solution(mesh):
    return jax.shard_map(
        body,
        mesh=mesh,
        in_specs=(
            P("chan", "tm"),
            P(),
            P(),
            P("chan", None, None),
            P(None, "tm", None),
            P(None, "tm"),
        ),
        out_specs=P("chan", "tm", None, None, None, None),
        check_vma=False,
    )
```

```python
import functools

import jax
import jax.numpy as jnp
from jax import lax
from jax.experimental import pallas as pl
from jax.experimental.pallas import tpu as pltpu
from jax.sharding import PartitionSpec as P

SEGLEN = 512
PRE = 128
LANES = 128
TILE = 16
GROUP = 256
SLOT_ROWS = 8
MESH = pl.DeviceIdType.MESH


def round_up(value, step):
    return -(-value // step) * step


def iota(shape, axis):
    return lax.broadcasted_iota(jnp.int32, shape, axis)


def kernel(
    owners, shards, x_ref, taps_hbm, map_hbm, cross_hbm, starts_ref, counts_ref, out_ref,
    held, taps_ref, map_ref, cross_ref, pack, arrived, placer, ordered, cross, table, rows_of, built,
    load_sem, small_sem, chan_send, chan_recv, tail_send, tail_recv, out_sem,
):
    me = lax.axis_index("chan")
    shard = lax.axis_index("tm")
    rows, samples = x_ref.shape
    klen = taps_ref.shape[1]
    sig, crystals = cross_ref.shape[0], cross_ref.shape[1]
    main = 2 * TILE
    rest = sig - main
    groups = TILE // rest
    slot = round_up(sig, SLOT_ROWS)
    height = crystals * slot
    blocks = (samples + klen) // LANES
    half_blocks = klen // LANES
    later = shard < shards - 1

    def load(half):
        return pltpu.make_async_copy(
            x_ref.at[:, half * klen : (half + 1) * klen], held.at[half], load_sem.at[half]
        )

    small = [
        pltpu.make_async_copy(source, target, small_sem.at[at])
        for at, (source, target) in enumerate(
            [(taps_hbm, taps_ref), (map_hbm, map_ref), (cross_hbm, cross_ref)]
        )
    ]
    load(1).start()
    load(0).start()
    for copy in small:
        copy.start()

    def partner(step):
        if owners & (owners - 1) == 0:
            return me ^ step, me ^ step
        return lax.rem(me + step, owners), lax.rem(me + owners - step, owners)

    steps = [step for low in range(2) for step in range(low, owners, 2)]
    steps = [1] + [step for step in steps if step > 1] if owners > 1 else []

    barrier = pltpu.get_barrier_semaphore()
    for step in range(1, owners):
        pl.semaphore_signal(
            barrier, inc=1, device_id={"chan": partner(step)[0]}, device_id_type=MESH
        )

    @pl.when(shard > 0)
    def _():
        pl.semaphore_signal(barrier, inc=1, device_id={"tm": shard - 1}, device_id_type=MESH)

    def rest_row(index):
        turned = index - main
        for group in range(1, groups):
            turned = turned - jnp.where(index >= main + group * rest, rest, 0)
        return jnp.where(index < main, index, main + turned)

    def pack_half(half):
        load(half).wait()
        for owner in range(owners):
            base = owner * sig
            low = base // TILE * TILE
            high = min(round_up(base + sig, TILE), rows)
            shape = (main + TILE, high - low)
            index = iota(shape, 0)
            wanted = base + rest_row(index)
            hit = jnp.logical_and(iota(shape, 1) + low == wanted, index < main + groups * rest)
            picker = jnp.where(hit, 1.0, 0.0).astype(jnp.bfloat16)
            picked = jnp.dot(picker, held[half, low:high, :], preferred_element_type=jnp.float32)
            pack[half, owner, :, 0:klen] = picked[0:TILE].astype(jnp.bfloat16)
            pack[half, owner, :, klen : 2 * klen] = picked[TILE:main].astype(jnp.bfloat16)
            left = picked[main:]
            last = left[:, 2 * GROUP : klen]
            row = iota((TILE, GROUP), 0)
            kept = jnp.where(
                row < rest,
                left[:, 0:GROUP],
                jnp.where(row < 2 * rest, left[:, GROUP : 2 * GROUP], jnp.concatenate([last, last], axis=1)),
            )
            pack[half, owner, :, 2 * klen : 2 * klen + GROUP] = kept.astype(jnp.bfloat16)
        arrived[half + 1, me] = pack[half, me]

    pack_half(1)

    @pl.when(shard == 0)
    def _():
        arrived[0] = jnp.zeros(arrived.shape[1:], arrived.dtype)

    pl.semaphore_wait(barrier, owners - 1 + jnp.where(later, 1, 0))

    def to_owner(half, step):
        peer = partner(step)[0]
        return pltpu.make_async_remote_copy(
            src_ref=pack.at[half, peer],
            dst_ref=arrived.at[half + 1, me],
            send_sem=chan_send.at[half, step],
            recv_sem=chan_recv.at[half, step],
            device_id={"chan": peer},
            device_id_type=MESH,
        )

    def from_owner(half, step):
        peer = partner(step)[1]
        return pltpu.make_async_remote_copy(
            src_ref=pack.at[half, peer],
            dst_ref=arrived.at[half + 1, peer],
            send_sem=chan_send.at[half, step],
            recv_sem=chan_recv.at[half, step],
            device_id={"chan": peer},
            device_id_type=MESH,
        )

    def onward(step):
        peer = partner(step)[1] if step else me
        return pltpu.make_async_remote_copy(
            src_ref=arrived.at[2, peer],
            dst_ref=arrived.at[0, peer],
            send_sem=tail_send.at[step],
            recv_sem=tail_recv.at[step],
            device_id={"tm": jnp.minimum(shard + 1, shards - 1)},
            device_id_type=MESH,
        )

    for step in steps:
        to_owner(1, step).start()

    @pl.when(later)
    def _():
        onward(0).start()

    pack_half(0)
    for step in steps:
        to_owner(0, step).start()

    for copy in small:
        copy.wait()

    taps = taps_ref[...].astype(jnp.float32)
    square = (LANES, LANES)
    upper = iota(square, 1) >= iota(square, 0)
    nothing = jnp.zeros(square, jnp.float32)
    for filter_index in range(taps.shape[0]):
        turned = []
        for block in range(half_blocks):
            row = taps[filter_index : filter_index + 1, block * LANES : (block + 1) * LANES]
            turned.append(pltpu.roll(jnp.broadcast_to(row, square), 0, 1, stride=1, stride_axis=0))
        turned.append(nothing)
        for block in range(half_blocks + 1):
            above = turned[half_blocks - block]
            below = turned[half_blocks - 1 - block] if block < half_blocks else nothing
            table[
                block * LANES : (block + 1) * LANES,
                filter_index * LANES : (filter_index + 1) * LANES,
            ] = jnp.where(upper, above, below).astype(table.dtype)

    for step in steps:
        from_owner(1, step).wait_recv()

        @pl.when(later)
        def _():
            onward(step).start()

    columns = []
    total = map_ref.shape[0]
    for source in range(owners):
        low = source * rows // LANES * LANES
        high = min(round_up((source + 1) * rows, LANES), total)
        shape = (main + TILE, high - low)
        index = iota(shape, 0)
        wanted = source * rows + me * sig + rest_row(index)
        hit = jnp.logical_and(iota(shape, 1) + low == wanted, index < main + groups * rest)
        names = (map_ref[low:high].astype(jnp.float32) + 1.0).reshape(1, high - low)
        columns.append(jnp.sum(jnp.where(hit, names, 0.0), axis=1, keepdims=True))
    column = jnp.concatenate(
        [c[0:TILE] for c in columns] + [c[TILE:main] for c in columns] + [c[main:] for c in columns],
        axis=0,
    )
    depth = owners * (main + TILE)
    width = round_up(height, LANES)
    lane = iota((1, width), 1)
    crystal_of = jnp.zeros((1, width), jnp.int32)
    for crystal in range(1, crystals):
        crystal_of = crystal_of + jnp.where(lane >= crystal * slot, 1, 0)
    signal_of = lane - crystal_of * slot
    wanted = jnp.where(signal_of < sig, crystal_of * sig + signal_of + me * rows + 1, -1)
    matched = jnp.where(column == wanted.astype(jnp.float32), 1.0, 0.0)
    turned = jnp.transpose(matched)[0:height]
    cross[...] = jnp.zeros(cross.shape, cross.dtype)
    cross[0 : sig * crystals, 0:sig] = cross_ref[...].astype(jnp.float32).reshape(sig * crystals, sig)
    lane = iota((height, depth), 1)
    part_of = jnp.where(lane < owners * main, -1, lane & (TILE - 1))
    for group in range(groups):
        own = jnp.logical_and(part_of >= group * rest, part_of < (group + 1) * rest)
        keep = jnp.logical_or(part_of < 0, own)
        placer[group] = jnp.where(keep, turned, 0.0).astype(placer.dtype)

    def place(part, first_block):
        source = arrived[part].reshape(owners * TILE, arrived.shape[3])
        for group in range(groups):
            low = group * GROUP
            high = min(low + GROUP, klen)
            stacked = jnp.concatenate(
                [
                    source[:, low:high],
                    source[:, klen + low : klen + high],
                    source[:, 2 * klen : 2 * klen + high - low],
                ],
                axis=0,
            )
            rows_out = jnp.dot(placer[group], stacked, preferred_element_type=jnp.float32)
            for block in range((high - low) // LANES):
                ordered[first_block + low // LANES + block] = rows_out[
                    :, block * LANES : (block + 1) * LANES
                ]

    place(2, 2 * half_blocks)
    for step in steps:
        from_owner(0, step).wait_recv()
    place(1, half_blocks)

    @pl.when(shard > 0)
    def _():
        for step in range(owners):
            onward(step).wait_recv()

    place(0, 0)
    ordered[blocks] = jnp.zeros(ordered.shape[1:], ordered.dtype)

    filters = taps.shape[0]
    window_blocks = (SEGLEN + klen) // LANES
    seg_blocks = SEGLEN // LANES
    steps_back = half_blocks + 1
    lane = iota((slot, LANES), 1)
    center = (PRE - 1) / 2.0
    fit_axis = [
        (iota((1, LANES), 1).astype(jnp.float32) + (block * LANES - center)) / (PRE / 2.0)
        for block in range(seg_blocks)
    ]
    pre_axis = fit_axis[0]
    power = jnp.sum(pre_axis * pre_axis)
    taps_table = table[...]
    pair = 2 if crystals % 2 == 0 else 1
    high = pair * slot
    for crystal in range(0, crystals, pair):
        windows = []
        for member in range(crystal, crystal + pair):
            start = starts_ref[me * crystals + member]
            first = start >> 7
            shift = start & (LANES - 1)
            back = (LANES - shift) & (LANES - 1)
            at = slice(member * slot, (member + 1) * slot)
            rolled = [
                pltpu.roll(ordered[first + block, at, :], back, 1)
                for block in range(window_blocks + 1)
            ]
            windows.append(
                [
                    jnp.where(lane < LANES - shift, rolled[block], rolled[block + 1])
                    for block in range(window_blocks)
                ]
            )
        cut = [
            jnp.concatenate([w[block] for w in windows], axis=0).astype(jnp.bfloat16)
            for block in range(window_blocks)
        ]
        wide = jnp.concatenate(
            [jnp.concatenate(cut[b : b + steps_back], axis=1) for b in range(seg_blocks)], axis=0
        )
        filtered = jnp.dot(wide, taps_table, preferred_element_type=jnp.float32)
        for member in range(pair):
            at = crystal + member
            live = counts_ref[me * crystals + at] > 0
            pieces = jnp.concatenate(
                [
                    filtered[b * high + member * slot : b * high + (member + 1) * slot]
                    for b in range(seg_blocks)
                ],
                axis=1,
            ).astype(jnp.bfloat16)
            mixer = cross[pl.ds(at, slot, stride=crystals), :][:, 0:slot].astype(jnp.bfloat16)
            coupled = pieces.astype(jnp.float32) + jnp.dot(
                mixer, pieces, preferred_element_type=jnp.float32
            )
            for filter_index in range(filters):
                own = [
                    coupled[:, (b * filters + filter_index) * LANES :][:, :LANES]
                    for b in range(seg_blocks)
                ]
                offset_fit = jnp.mean(own[0], axis=1, keepdims=True)
                slope_fit = jnp.sum(own[0] * pre_axis, axis=1, keepdims=True) / power
                for b in range(seg_blocks):
                    fitted = own[b] - offset_fit - slope_fit * fit_axis[b]
                    rows_of[
                        at, pl.ds(b * filters + filter_index, slot, stride=filters * seg_blocks), :
                    ] = jnp.where(live, fitted, 0.0)
            built[at] = rows_of[at, 0 : built.shape[1], :].astype(built.dtype)
            pltpu.make_async_copy(built.at[at], out_ref.at[at], out_sem.at[at]).start()
    for step in steps:
        to_owner(1, step).wait_send()
        to_owner(0, step).wait_send()

    @pl.when(later)
    def _():
        for step in range(owners):
            onward(step).wait_send()
    for at in range(crystals):
        pltpu.make_async_copy(built.at[at], out_ref.at[at], out_sem.at[at]).wait()


def body(signals, kernels, chan_map, crosstalk, starts, counts):
    owners = lax.axis_size("chan")
    shards = lax.axis_size("tm")
    rows, samples = signals.shape
    filters, klen = kernels.shape
    crystals, sig, _ = crosstalk.shape
    slots = starts.shape[2]
    slot = round_up(sig, SLOT_ROWS)
    height = crystals * slot
    packed = 2 * klen + GROUP
    blocks = SEGLEN // LANES
    in_smem = pl.BlockSpec(memory_space=pltpu.SMEM)
    in_hbm = pl.BlockSpec(memory_space=pltpu.HBM)
    built = pl.pallas_call(
        functools.partial(kernel, owners, shards),
        out_shape=jax.ShapeDtypeStruct((crystals, sig * blocks * filters, LANES), jnp.bfloat16),
        in_specs=[in_hbm] * 4 + [in_smem] * 2,
        out_specs=in_hbm,
        scratch_shapes=[
            pltpu.VMEM((2, rows, klen), jnp.bfloat16),
            pltpu.VMEM(kernels.shape, kernels.dtype),
            pltpu.VMEM(chan_map.shape, chan_map.dtype),
            pltpu.VMEM((sig, crystals, sig), crosstalk.dtype),
            pltpu.VMEM((2, owners, TILE, packed), jnp.bfloat16),
            pltpu.VMEM((3, owners, TILE, packed), jnp.bfloat16),
            pltpu.VMEM((TILE // (sig - 2 * TILE), height, owners * 3 * TILE), jnp.bfloat16),
            pltpu.VMEM(((samples + klen) // LANES + 1, height, LANES), jnp.float32),
            pltpu.VMEM((height, LANES), jnp.float32),
            pltpu.VMEM((klen + LANES, filters * LANES), jnp.bfloat16),
            pltpu.VMEM((crystals, slot * blocks * filters, LANES), jnp.float32),
            pltpu.VMEM((crystals, sig * blocks * filters, LANES), jnp.bfloat16),
            pltpu.SemaphoreType.DMA((2,)),
            pltpu.SemaphoreType.DMA((3,)),
            pltpu.SemaphoreType.DMA((2, owners)),
            pltpu.SemaphoreType.DMA((2, owners)),
            pltpu.SemaphoreType.DMA((owners,)),
            pltpu.SemaphoreType.DMA((owners,)),
            pltpu.SemaphoreType.DMA((crystals,)),
        ],
        compiler_params=pltpu.CompilerParams(
            collective_id=0, has_side_effects=True, vmem_limit_bytes=62 * 1024 * 1024
        ),
        name="build_events",
    )(
        signals,
        kernels,
        chan_map,
        jnp.transpose(crosstalk, (1, 0, 2)),
        starts.reshape(-1),
        counts.reshape(-1),
    )
    parts = built.reshape(crystals, sig, blocks, filters, LANES)
    return jnp.transpose(parts, (0, 3, 1, 2, 4)).reshape(crystals, 1, slots, filters, sig, SEGLEN)


def solution(mesh):
    return jax.shard_map(
        body,
        mesh=mesh,
        in_specs=(
            P("chan", "tm"),
            P(),
            P(),
            P("chan", None, None),
            P(None, "tm", None),
            P(None, "tm"),
        ),
        out_specs=P("chan", "tm", None, None, None, None),
        check_vma=False,
    )
```

```python
import functools

import jax
import jax.numpy as jnp
from jax import lax
from jax.experimental import pallas as pl
from jax.experimental.pallas import tpu as pltpu
from jax.sharding import PartitionSpec as P

SEGLEN = 512
PRE = 128
LANES = 128
TILE = 16
GROUP = 256
SLOT_ROWS = 8
VMEM_BYTES = 56 * 1024 * 1024
MESH = pl.DeviceIdType.MESH


def round_up(value, step):
    return -(-value // step) * step


def iota(shape, axis):
    return lax.broadcasted_iota(jnp.int32, shape, axis)


def gather_kernel(
    owners, shards, x_ref, taps_hbm, map_hbm, cross_hbm, starts_ref, counts_ref,
    ordered, table, coupling, plan,
    held, taps_ref, map_ref, cross_ref, pack, arrived, placer, cross,
    load_sem, small_sem, chan_send, chan_recv, tail_send, tail_recv,
):
    me = lax.axis_index("chan")
    shard = lax.axis_index("tm")
    rows, samples = x_ref.shape
    klen = taps_ref.shape[1]
    sig, crystals = cross_ref.shape[0], cross_ref.shape[1]
    main = 2 * TILE
    rest = sig - main
    groups = TILE // rest
    slot = round_up(sig, SLOT_ROWS)
    height = crystals * slot
    blocks = (samples + klen) // LANES
    half_blocks = klen // LANES
    later = shard < shards - 1

    def load(half):
        return pltpu.make_async_copy(
            x_ref.at[:, half * klen : (half + 1) * klen], held.at[half], load_sem.at[half]
        )

    small = [
        pltpu.make_async_copy(source, target, small_sem.at[at])
        for at, (source, target) in enumerate(
            [(taps_hbm, taps_ref), (map_hbm, map_ref), (cross_hbm, cross_ref)]
        )
    ]
    load(1).start()
    load(0).start()
    for copy in small:
        copy.start()

    def partner(step):
        if owners & (owners - 1) == 0:
            return me ^ step, me ^ step
        return lax.rem(me + step, owners), lax.rem(me + owners - step, owners)

    steps = [step for low in range(2) for step in range(low, owners, 2)]
    steps = [1] + [step for step in steps if step > 1] if owners > 1 else []

    barrier = pltpu.get_barrier_semaphore()
    for step in range(1, owners):
        pl.semaphore_signal(
            barrier, inc=1, device_id={"chan": partner(step)[0]}, device_id_type=MESH
        )

    @pl.when(shard > 0)
    def _():
        pl.semaphore_signal(barrier, inc=1, device_id={"tm": shard - 1}, device_id_type=MESH)

    def rest_row(index):
        turned = index - main
        for group in range(1, groups):
            turned = turned - jnp.where(index >= main + group * rest, rest, 0)
        return jnp.where(index < main, index, main + turned)

    def pack_half(half):
        load(half).wait()
        for owner in range(owners):
            base = owner * sig
            low = base // TILE * TILE
            high = min(round_up(base + sig, TILE), rows)
            shape = (main + TILE, high - low)
            index = iota(shape, 0)
            wanted = base + rest_row(index)
            hit = jnp.logical_and(iota(shape, 1) + low == wanted, index < main + groups * rest)
            picker = jnp.where(hit, 1.0, 0.0).astype(jnp.bfloat16)
            picked = jnp.dot(picker, held[half, low:high, :], preferred_element_type=jnp.float32)
            pack[half, owner, :, 0:klen] = picked[0:TILE].astype(jnp.bfloat16)
            pack[half, owner, :, klen : 2 * klen] = picked[TILE:main].astype(jnp.bfloat16)
            left = picked[main:]
            last = left[:, 2 * GROUP : klen]
            row = iota((TILE, GROUP), 0)
            kept = jnp.where(
                row < rest,
                left[:, 0:GROUP],
                jnp.where(row < 2 * rest, left[:, GROUP : 2 * GROUP], jnp.concatenate([last, last], axis=1)),
            )
            pack[half, owner, :, 2 * klen : 2 * klen + GROUP] = kept.astype(jnp.bfloat16)
        arrived[half + 1, me] = pack[half, me]

    pack_half(1)

    @pl.when(shard == 0)
    def _():
        arrived[0] = jnp.zeros(arrived.shape[1:], arrived.dtype)

    pl.semaphore_wait(barrier, owners - 1 + jnp.where(later, 1, 0))

    def to_owner(half, step):
        peer = partner(step)[0]
        return pltpu.make_async_remote_copy(
            src_ref=pack.at[half, peer],
            dst_ref=arrived.at[half + 1, me],
            send_sem=chan_send.at[half, step],
            recv_sem=chan_recv.at[half, step],
            device_id={"chan": peer},
            device_id_type=MESH,
        )

    def from_owner(half, step):
        peer = partner(step)[1]
        return pltpu.make_async_remote_copy(
            src_ref=pack.at[half, peer],
            dst_ref=arrived.at[half + 1, peer],
            send_sem=chan_send.at[half, step],
            recv_sem=chan_recv.at[half, step],
            device_id={"chan": peer},
            device_id_type=MESH,
        )

    def onward(step):
        peer = partner(step)[1] if step else me
        return pltpu.make_async_remote_copy(
            src_ref=arrived.at[2, peer],
            dst_ref=arrived.at[0, peer],
            send_sem=tail_send.at[step],
            recv_sem=tail_recv.at[step],
            device_id={"tm": jnp.minimum(shard + 1, shards - 1)},
            device_id_type=MESH,
        )

    for step in steps:
        to_owner(1, step).start()

    @pl.when(later)
    def _():
        onward(0).start()

    pack_half(0)
    for step in steps:
        to_owner(0, step).start()

    for copy in small:
        copy.wait()

    taps = taps_ref[...].astype(jnp.float32)
    square = (LANES, LANES)
    upper = iota(square, 1) >= iota(square, 0)
    nothing = jnp.zeros(square, jnp.float32)
    for filter_index in range(taps.shape[0]):
        turned = []
        for block in range(half_blocks):
            row = taps[filter_index : filter_index + 1, block * LANES : (block + 1) * LANES]
            turned.append(pltpu.roll(jnp.broadcast_to(row, square), 0, 1, stride=1, stride_axis=0))
        turned.append(nothing)
        for block in range(half_blocks + 1):
            above = turned[half_blocks - block]
            below = turned[half_blocks - 1 - block] if block < half_blocks else nothing
            table[
                block * LANES : (block + 1) * LANES,
                filter_index * LANES : (filter_index + 1) * LANES,
            ] = jnp.where(upper, above, below).astype(table.dtype)

    for step in steps:
        from_owner(1, step).wait_recv()

        @pl.when(later)
        def _():
            onward(step).start()

    columns = []
    total = map_ref.shape[0]
    for source in range(owners):
        low = source * rows // LANES * LANES
        high = min(round_up((source + 1) * rows, LANES), total)
        shape = (main + TILE, high - low)
        index = iota(shape, 0)
        wanted = source * rows + me * sig + rest_row(index)
        hit = jnp.logical_and(iota(shape, 1) + low == wanted, index < main + groups * rest)
        names = (map_ref[low:high].astype(jnp.float32) + 1.0).reshape(1, high - low)
        columns.append(jnp.sum(jnp.where(hit, names, 0.0), axis=1, keepdims=True))
    column = jnp.concatenate(
        [c[0:TILE] for c in columns] + [c[TILE:main] for c in columns] + [c[main:] for c in columns],
        axis=0,
    )
    depth = owners * (main + TILE)
    width = round_up(height, LANES)
    lane = iota((1, width), 1)
    crystal_of = jnp.zeros((1, width), jnp.int32)
    for crystal in range(1, crystals):
        crystal_of = crystal_of + jnp.where(lane >= crystal * slot, 1, 0)
    signal_of = lane - crystal_of * slot
    wanted = jnp.where(signal_of < sig, crystal_of * sig + signal_of + me * rows + 1, -1)
    matched = jnp.where(column == wanted.astype(jnp.float32), 1.0, 0.0)
    turned = jnp.transpose(matched)[0:height]
    lane = iota((1, LANES), 1)
    begins = jnp.zeros((1, LANES), jnp.int32)
    lives = jnp.zeros((1, LANES), jnp.int32)
    for crystal in range(crystals):
        begins = jnp.where(lane == crystal, starts_ref[me * crystals + crystal], begins)
        lives = jnp.where(lane == crystal, counts_ref[me * crystals + crystal], lives)
    plan[0:1] = begins
    plan[1:2] = lives

    cross[...] = jnp.zeros(cross.shape, cross.dtype)
    cross[0 : sig * crystals, 0:sig] = cross_ref[...].astype(jnp.float32).reshape(sig * crystals, sig)
    for crystal in range(crystals):
        coupling[crystal] = cross[pl.ds(crystal, slot, stride=crystals), :]
    lane = iota((height, depth), 1)
    part_of = jnp.where(lane < owners * main, -1, lane & (TILE - 1))
    for group in range(groups):
        own = jnp.logical_and(part_of >= group * rest, part_of < (group + 1) * rest)
        keep = jnp.logical_or(part_of < 0, own)
        placer[group] = jnp.where(keep, turned, 0.0).astype(placer.dtype)

    def place(part, first_block):
        source = arrived[part].reshape(owners * TILE, arrived.shape[3])
        for group in range(groups):
            low = group * GROUP
            high = min(low + GROUP, klen)
            stacked = jnp.concatenate(
                [
                    source[:, low:high],
                    source[:, klen + low : klen + high],
                    source[:, 2 * klen : 2 * klen + high - low],
                ],
                axis=0,
            )
            rows_out = jnp.dot(placer[group], stacked, preferred_element_type=jnp.float32)
            for block in range((high - low) // LANES):
                ordered[first_block + low // LANES + block] = rows_out[
                    :, block * LANES : (block + 1) * LANES
                ]

    place(2, 2 * half_blocks)
    for step in steps:
        from_owner(0, step).wait_recv()
    place(1, half_blocks)

    @pl.when(shard > 0)
    def _():
        for step in range(owners):
            onward(step).wait_recv()

    place(0, 0)
    ordered[blocks] = jnp.zeros(ordered.shape[1:], ordered.dtype)

    for step in steps:
        to_owner(1, step).wait_send()
        to_owner(0, step).wait_send()

    @pl.when(later)
    def _():
        for step in range(owners):
            onward(step).wait_send()


def build_kernel(
    sig, ordered, table, coupling, plan, out_ref, rows_of, built, out_sem
):
    crystals, slot = coupling.shape[0], coupling.shape[1]
    filters = table.shape[1] // LANES
    half_blocks = table.shape[0] // LANES - 1
    klen = half_blocks * LANES

    window_blocks = (SEGLEN + klen) // LANES
    seg_blocks = SEGLEN // LANES
    steps_back = half_blocks + 1
    lane = iota((slot, LANES), 1)
    center = (PRE - 1) / 2.0
    fit_axis = [
        (iota((1, LANES), 1).astype(jnp.float32) + (block * LANES - center)) / (PRE / 2.0)
        for block in range(seg_blocks)
    ]
    pre_axis = fit_axis[0]
    power = jnp.sum(pre_axis * pre_axis)
    taps_table = table[...]
    pair = 2 if crystals % 2 == 0 else 1
    high = pair * slot
    for crystal in range(0, crystals, pair):
        windows = []
        for member in range(crystal, crystal + pair):
            start = plan[0, member]
            first = start >> 7
            shift = start & (LANES - 1)
            back = (LANES - shift) & (LANES - 1)
            at = slice(member * slot, (member + 1) * slot)
            rolled = [
                pltpu.roll(ordered[first + block, at, :], back, 1)
                for block in range(window_blocks + 1)
            ]
            windows.append(
                [
                    jnp.where(lane < LANES - shift, rolled[block], rolled[block + 1])
                    for block in range(window_blocks)
                ]
            )
        cut = [
            jnp.concatenate([w[block] for w in windows], axis=0).astype(jnp.bfloat16)
            for block in range(window_blocks)
        ]
        wide = jnp.concatenate(
            [jnp.concatenate(cut[b : b + steps_back], axis=1) for b in range(seg_blocks)], axis=0
        )
        filtered = jnp.dot(wide, taps_table, preferred_element_type=jnp.float32)
        for member in range(pair):
            at = crystal + member
            live = plan[1, at] > 0
            pieces = jnp.concatenate(
                [
                    filtered[b * high + member * slot : b * high + (member + 1) * slot]
                    for b in range(seg_blocks)
                ],
                axis=1,
            ).astype(jnp.bfloat16)
            mixer = coupling[at][:, 0:slot].astype(jnp.bfloat16)
            coupled = pieces.astype(jnp.float32) + jnp.dot(
                mixer, pieces, preferred_element_type=jnp.float32
            )
            for filter_index in range(filters):
                own = [
                    coupled[:, (b * filters + filter_index) * LANES :][:, :LANES]
                    for b in range(seg_blocks)
                ]
                offset_fit = jnp.mean(own[0], axis=1, keepdims=True)
                slope_fit = jnp.sum(own[0] * pre_axis, axis=1, keepdims=True) / power
                for b in range(seg_blocks):
                    fitted = own[b] - offset_fit - slope_fit * fit_axis[b]
                    rows_of[
                        at, pl.ds(b * filters + filter_index, slot, stride=filters * seg_blocks), :
                    ] = jnp.where(live, fitted, 0.0)
            built[at] = rows_of[at, 0 : built.shape[1], :].astype(built.dtype)
            pltpu.make_async_copy(built.at[at], out_ref.at[at], out_sem.at[at]).start()
    for at in range(crystals):
        pltpu.make_async_copy(built.at[at], out_ref.at[at], out_sem.at[at]).wait()


def body(signals, kernels, chan_map, crosstalk, starts, counts):
    owners = lax.axis_size("chan")
    shards = lax.axis_size("tm")
    rows, samples = signals.shape
    filters, klen = kernels.shape
    crystals, sig, _ = crosstalk.shape
    slots = starts.shape[2]
    slot = round_up(sig, SLOT_ROWS)
    height = crystals * slot
    packed = 2 * klen + GROUP
    blocks = SEGLEN // LANES
    in_vmem = pl.BlockSpec(memory_space=pltpu.VMEM)
    in_smem = pl.BlockSpec(memory_space=pltpu.SMEM)
    in_hbm = pl.BlockSpec(memory_space=pltpu.HBM)
    ordered, table, coupling, plan = pl.pallas_call(
        functools.partial(gather_kernel, owners, shards),
        out_shape=(
            pltpu.VMEM(((samples + klen) // LANES + 1, height, LANES), jnp.float32),
            pltpu.VMEM((klen + LANES, filters * LANES), jnp.bfloat16),
            pltpu.VMEM((crystals, slot, LANES), jnp.float32),
            pltpu.VMEM((2, LANES), jnp.int32),
        ),
        in_specs=[in_hbm] * 4 + [in_smem] * 2,
        out_specs=(in_vmem,) * 4,
        scratch_shapes=[
            pltpu.VMEM((2, rows, klen), jnp.bfloat16),
            pltpu.VMEM(kernels.shape, kernels.dtype),
            pltpu.VMEM(chan_map.shape, chan_map.dtype),
            pltpu.VMEM((sig, crystals, sig), crosstalk.dtype),
            pltpu.VMEM((2, owners, TILE, packed), jnp.bfloat16),
            pltpu.VMEM((3, owners, TILE, packed), jnp.bfloat16),
            pltpu.VMEM((TILE // (sig - 2 * TILE), height, owners * 3 * TILE), jnp.bfloat16),
            pltpu.VMEM((height, LANES), jnp.float32),
            pltpu.SemaphoreType.DMA((2,)),
            pltpu.SemaphoreType.DMA((3,)),
            pltpu.SemaphoreType.DMA((2, owners)),
            pltpu.SemaphoreType.DMA((2, owners)),
            pltpu.SemaphoreType.DMA((owners,)),
            pltpu.SemaphoreType.DMA((owners,)),
        ],
        compiler_params=pltpu.CompilerParams(
            collective_id=0, has_side_effects=True, vmem_limit_bytes=VMEM_BYTES
        ),
        name="gather_rows",
    )(
        signals,
        kernels,
        chan_map,
        jnp.transpose(crosstalk, (1, 0, 2)),
        starts.reshape(-1),
        counts.reshape(-1),
    )
    built = pl.pallas_call(
        functools.partial(build_kernel, sig),
        out_shape=jax.ShapeDtypeStruct((crystals, sig * blocks * filters, LANES), jnp.bfloat16),
        in_specs=[in_vmem] * 3 + [in_smem],
        out_specs=in_hbm,
        scratch_shapes=[
            pltpu.VMEM((crystals, slot * blocks * filters, LANES), jnp.float32),
            pltpu.VMEM((crystals, sig * blocks * filters, LANES), jnp.bfloat16),
            pltpu.SemaphoreType.DMA((crystals,)),
        ],
        compiler_params=pltpu.CompilerParams(vmem_limit_bytes=24 * 1024 * 1024),
        name="build_events",
    )(ordered, table, coupling, plan)
    parts = built.reshape(crystals, sig, blocks, filters, LANES)
    return jnp.transpose(parts, (0, 3, 1, 2, 4)).reshape(crystals, 1, slots, filters, sig, SEGLEN)


def solution(mesh):
    return jax.shard_map(
        body,
        mesh=mesh,
        in_specs=(
            P("chan", "tm"),
            P(),
            P(),
            P("chan", None, None),
            P(None, "tm", None),
            P(None, "tm"),
        ),
        out_specs=P("chan", "tm", None, None, None, None),
        check_vma=False,
    )
```

```python
import functools

import jax
import jax.numpy as jnp
from jax import lax
from jax.experimental import pallas as pl
from jax.experimental.pallas import tpu as pltpu
from jax.sharding import PartitionSpec as P

SEGLEN = 512
PRE = 128
LANES = 128
TILE = 16
GROUP = 256
SLOT_ROWS = 8
VMEM_BYTES = 56 * 1024 * 1024
MESH = pl.DeviceIdType.MESH


def round_up(value, step):
    return -(-value // step) * step


def iota(shape, axis):
    return lax.broadcasted_iota(jnp.int32, shape, axis)


def gather_kernel(
    owners, shards, x_ref, taps_hbm, map_hbm, cross_hbm, starts_ref, counts_ref,
    ordered, table, coupling, plan,
    held, taps_ref, map_ref, cross_ref, pack, arrived, placer, slots_ref, cross,
    load_sem, small_sem, chan_send, chan_recv, tail_send, tail_recv,
):
    me = lax.axis_index("chan")
    shard = lax.axis_index("tm")
    rows, samples = x_ref.shape
    klen = taps_ref.shape[1]
    sig, crystals = cross_ref.shape[0], cross_ref.shape[1]
    main = 2 * TILE
    rest = sig - main
    groups = TILE // rest
    slot = round_up(sig, SLOT_ROWS)
    height = crystals * slot
    blocks = (samples + klen) // LANES
    half_blocks = klen // LANES
    later = shard < shards - 1

    def load(half):
        return pltpu.make_async_copy(
            x_ref.at[:, half * klen : (half + 1) * klen], held.at[half], load_sem.at[half]
        )

    small = [
        pltpu.make_async_copy(source, target, small_sem.at[at])
        for at, (source, target) in enumerate(
            [(taps_hbm, taps_ref), (map_hbm, map_ref), (cross_hbm, cross_ref)]
        )
    ]
    load(1).start()
    load(0).start()
    for copy in small:
        copy.start()

    def partner(step):
        if owners & (owners - 1) == 0:
            return me ^ step, me ^ step
        return lax.rem(me + step, owners), lax.rem(me + owners - step, owners)

    steps = [step for low in range(2) for step in range(low, owners, 2)]
    steps = [1] + [step for step in steps if step > 1] if owners > 1 else []
    place_of = {step: at for at, step in enumerate([0] + steps)}
    splits = 2
    share = owners // splits
    span = share * (main + TILE)
    depth = round_up(span, LANES)

    barrier = pltpu.get_barrier_semaphore()
    for step in range(1, owners):
        pl.semaphore_signal(
            barrier, inc=1, device_id={"chan": partner(step)[0]}, device_id_type=MESH
        )

    @pl.when(shard > 0)
    def _():
        pl.semaphore_signal(barrier, inc=1, device_id={"tm": shard - 1}, device_id_type=MESH)

    def rest_row(index):
        turned = index - main
        for group in range(1, groups):
            turned = turned - jnp.where(index >= main + group * rest, rest, 0)
        return jnp.where(index < main, index, main + turned)

    def pack_half(half):
        load(half).wait()
        for owner in range(owners):
            base = owner * sig
            low = base // TILE * TILE
            high = min(round_up(base + sig, TILE), rows)
            shape = (main + TILE, high - low)
            index = iota(shape, 0)
            wanted = base + rest_row(index)
            hit = jnp.logical_and(iota(shape, 1) + low == wanted, index < main + groups * rest)
            picker = jnp.where(hit, 1.0, 0.0).astype(jnp.bfloat16)
            picked = jnp.dot(picker, held[half, low:high, :], preferred_element_type=jnp.float32)
            pack[half, owner, :, 0:klen] = picked[0:TILE].astype(jnp.bfloat16)
            pack[half, owner, :, klen : 2 * klen] = picked[TILE:main].astype(jnp.bfloat16)
            left = picked[main:]
            last = left[:, 2 * GROUP : klen]
            row = iota((TILE, GROUP), 0)
            kept = jnp.where(
                row < rest,
                left[:, 0:GROUP],
                jnp.where(row < 2 * rest, left[:, GROUP : 2 * GROUP], jnp.concatenate([last, last], axis=1)),
            )
            pack[half, owner, :, 2 * klen : 2 * klen + GROUP] = kept.astype(jnp.bfloat16)
        arrived[half + 1, 0] = pack[half, me]

    pack_half(1)

    @pl.when(shard == 0)
    def _():
        arrived[0] = jnp.zeros(arrived.shape[1:], arrived.dtype)

    pl.semaphore_wait(barrier, owners - 1 + jnp.where(later, 1, 0))

    def to_owner(half, step):
        peer = partner(step)[0]
        return pltpu.make_async_remote_copy(
            src_ref=pack.at[half, peer],
            dst_ref=arrived.at[half + 1, place_of[step]],
            send_sem=chan_send.at[half, step],
            recv_sem=chan_recv.at[half, step],
            device_id={"chan": peer},
            device_id_type=MESH,
        )

    def from_owner(half, step):
        peer = partner(step)[1]
        return pltpu.make_async_remote_copy(
            src_ref=pack.at[half, peer],
            dst_ref=arrived.at[half + 1, place_of[step]],
            send_sem=chan_send.at[half, step],
            recv_sem=chan_recv.at[half, step],
            device_id={"chan": peer},
            device_id_type=MESH,
        )

    def onward(step):
        return pltpu.make_async_remote_copy(
            src_ref=arrived.at[2, place_of[step]],
            dst_ref=arrived.at[0, place_of[step]],
            send_sem=tail_send.at[step],
            recv_sem=tail_recv.at[step],
            device_id={"tm": jnp.minimum(shard + 1, shards - 1)},
            device_id_type=MESH,
        )

    for step in steps:
        to_owner(1, step).start()

    @pl.when(later)
    def _():
        onward(0).start()

    pack_half(0)
    for step in steps:
        to_owner(0, step).start()

    for copy in small:
        copy.wait()

    taps = taps_ref[...].astype(jnp.float32)
    square = (LANES, LANES)
    upper = iota(square, 1) >= iota(square, 0)
    nothing = jnp.zeros(square, jnp.float32)
    for filter_index in range(taps.shape[0]):
        turned = []
        for block in range(half_blocks):
            row = taps[filter_index : filter_index + 1, block * LANES : (block + 1) * LANES]
            turned.append(pltpu.roll(jnp.broadcast_to(row, square), 0, 1, stride=1, stride_axis=0))
        turned.append(nothing)
        for block in range(half_blocks + 1):
            above = turned[half_blocks - block]
            below = turned[half_blocks - 1 - block] if block < half_blocks else nothing
            table[
                block * LANES : (block + 1) * LANES,
                filter_index * LANES : (filter_index + 1) * LANES,
            ] = jnp.where(upper, above, below).astype(table.dtype)

    for step in steps:
        from_owner(1, step).wait_recv()

        @pl.when(later)
        def _():
            onward(step).start()

    slots_ref[...] = jnp.full(slots_ref.shape, -5.0, slots_ref.dtype)
    total = map_ref.shape[0]
    for source in range(owners):
        low = source * rows // LANES * LANES
        high = min(round_up((source + 1) * rows, LANES), total)
        shape = (main + TILE, high - low)
        index = iota(shape, 0)
        wanted = source * rows + me * sig + rest_row(index)
        hit = jnp.logical_and(iota(shape, 1) + low == wanted, index < main + groups * rest)
        names = (map_ref[low:high].astype(jnp.float32) + 1.0).reshape(1, high - low)
        column = jnp.sum(jnp.where(hit, names, 0.0), axis=1, keepdims=True)
        column = jnp.broadcast_to(column, (main + TILE, LANES))
        step_to = me ^ source if owners & (owners - 1) == 0 else lax.rem(me - source + owners, owners)
        at = 0
        for step, place_at in place_of.items():
            first = place_at // share * depth + place_at % share * TILE
            at = at + jnp.where(step_to == step, first, 0)
        for part in range(3):
            target = pl.ds(pl.multiple_of(at + part * share * TILE, TILE), TILE)
            slots_ref[target, :] = column[part * TILE : (part + 1) * TILE]
    column = slots_ref[:, 0:1]
    width = round_up(height, LANES)
    lane = iota((1, width), 1)
    crystal_of = jnp.zeros((1, width), jnp.int32)
    for crystal in range(1, crystals):
        crystal_of = crystal_of + jnp.where(lane >= crystal * slot, 1, 0)
    signal_of = lane - crystal_of * slot
    wanted = jnp.where(signal_of < sig, crystal_of * sig + signal_of + me * rows + 1, -1)
    matched = jnp.where(column == wanted.astype(jnp.float32), 1.0, 0.0)
    turned = jnp.transpose(matched)[0:height]
    lane = iota((1, LANES), 1)
    begins = jnp.zeros((1, LANES), jnp.int32)
    lives = jnp.zeros((1, LANES), jnp.int32)
    for crystal in range(crystals):
        begins = jnp.where(lane == crystal, starts_ref[me * crystals + crystal], begins)
        lives = jnp.where(lane == crystal, counts_ref[me * crystals + crystal], lives)
    plan[0:1] = begins
    plan[1:2] = lives

    cross[...] = jnp.zeros(cross.shape, cross.dtype)
    cross[0 : sig * crystals, 0:sig] = cross_ref[...].astype(jnp.float32).reshape(sig * crystals, sig)
    for crystal in range(crystals):
        coupling[crystal] = cross[pl.ds(crystal, slot, stride=crystals), :]
    lane = iota((height, depth), 1)
    part_of = jnp.where(lane < share * main, -1, lane & (TILE - 1))
    for group in range(groups):
        own = jnp.logical_and(part_of >= group * rest, part_of < (group + 1) * rest)
        keep = jnp.logical_or(part_of < 0, own)
        for split in range(splits):
            own = turned[:, split * depth : (split + 1) * depth]
            placer[split, group] = jnp.where(keep, own, 0.0).astype(placer.dtype)

    def place(part, first_block, split):
        source = arrived[part, split * share : (split + 1) * share]
        source = source.reshape(share * TILE, arrived.shape[3])
        for group in range(groups):
            low = group * GROUP
            high = min(low + GROUP, klen)
            stacked = jnp.concatenate(
                [
                    source[:, low:high],
                    source[:, klen + low : klen + high],
                    source[:, 2 * klen : 2 * klen + high - low],
                ],
                axis=0,
            )
            rows_out = jnp.dot(
                placer[split, group][:, 0:span], stacked, preferred_element_type=jnp.float32)
            for block in range((high - low) // LANES):
                at = first_block + low // LANES + block
                piece = rows_out[:, block * LANES : (block + 1) * LANES]
                ordered[at] = piece if split == 0 else ordered[at] + piece

    members = [[step for step in place_of if place_of[step] // share == split] for split in range(splits)]
    for split in range(splits):
        place(2, 2 * half_blocks, split)
    for split in range(splits):
        for step in members[split]:
            if step:
                from_owner(0, step).wait_recv()
        place(1, half_blocks, split)

        @pl.when(shard > 0)
        def _():
            for step in members[split]:
                onward(step).wait_recv()

        place(0, 0, split)
    ordered[blocks] = jnp.zeros(ordered.shape[1:], ordered.dtype)

    for step in steps:
        to_owner(1, step).wait_send()
        to_owner(0, step).wait_send()

    @pl.when(later)
    def _():
        for step in range(owners):
            onward(step).wait_send()


def build_kernel(
    sig, ordered, table, coupling, plan, out_ref, rows_of, built, out_sem
):
    crystals, slot = coupling.shape[0], coupling.shape[1]
    filters = table.shape[1] // LANES
    half_blocks = table.shape[0] // LANES - 1
    klen = half_blocks * LANES

    window_blocks = (SEGLEN + klen) // LANES
    seg_blocks = SEGLEN // LANES
    steps_back = half_blocks + 1
    lane = iota((slot, LANES), 1)
    center = (PRE - 1) / 2.0
    fit_axis = [
        (iota((1, LANES), 1).astype(jnp.float32) + (block * LANES - center)) / (PRE / 2.0)
        for block in range(seg_blocks)
    ]
    pre_axis = fit_axis[0]
    power = jnp.sum(pre_axis * pre_axis)
    taps_table = table[...]
    pair = 4 if crystals % 4 == 0 else 1
    high = pair * slot
    for crystal in range(0, crystals, pair):
        windows = []
        for member in range(crystal, crystal + pair):
            start = plan[0, member]
            first = start >> 7
            shift = start & (LANES - 1)
            back = (LANES - shift) & (LANES - 1)
            at = slice(member * slot, (member + 1) * slot)
            rolled = [
                pltpu.roll(ordered[first + block, at, :], back, 1)
                for block in range(window_blocks + 1)
            ]
            windows.append(
                [
                    jnp.where(lane < LANES - shift, rolled[block], rolled[block + 1])
                    for block in range(window_blocks)
                ]
            )
        cut = [
            jnp.concatenate([w[block] for w in windows], axis=0).astype(jnp.bfloat16)
            for block in range(window_blocks)
        ]
        wide = jnp.concatenate(
            [jnp.concatenate(cut[b : b + steps_back], axis=1) for b in range(seg_blocks)], axis=0
        )
        filtered = jnp.dot(wide, taps_table, preferred_element_type=jnp.float32)
        for member in range(pair):
            at = crystal + member
            live = plan[1, at] > 0
            pieces = jnp.concatenate(
                [
                    filtered[b * high + member * slot : b * high + (member + 1) * slot]
                    for b in range(seg_blocks)
                ],
                axis=1,
            ).astype(jnp.bfloat16)
            mixer = coupling[at][:, 0:slot].astype(jnp.bfloat16)
            coupled = pieces.astype(jnp.float32) + jnp.dot(
                mixer, pieces, preferred_element_type=jnp.float32
            )
            for filter_index in range(filters):
                own = [
                    coupled[:, (b * filters + filter_index) * LANES :][:, :LANES]
                    for b in range(seg_blocks)
                ]
                offset_fit = jnp.mean(own[0], axis=1, keepdims=True)
                slope_fit = jnp.sum(own[0] * pre_axis, axis=1, keepdims=True) / power
                for b in range(seg_blocks):
                    fitted = own[b] - offset_fit - slope_fit * fit_axis[b]
                    rows_of[
                        at, pl.ds(b * filters + filter_index, slot, stride=filters * seg_blocks), :
                    ] = jnp.where(live, fitted, 0.0)
        for at in range(crystal, crystal + pair):
            built[at] = rows_of[at, 0 : built.shape[1], :].astype(built.dtype)
        for at in range(crystal, crystal + pair):
            pltpu.make_async_copy(built.at[at], out_ref.at[at], out_sem.at[at]).start()
    for at in range(crystals):
        pltpu.make_async_copy(built.at[at], out_ref.at[at], out_sem.at[at]).wait()


def body(signals, kernels, chan_map, crosstalk, starts, counts):
    owners = lax.axis_size("chan")
    shards = lax.axis_size("tm")
    rows, samples = signals.shape
    filters, klen = kernels.shape
    crystals, sig, _ = crosstalk.shape
    slots = starts.shape[2]
    slot = round_up(sig, SLOT_ROWS)
    height = crystals * slot
    packed = 2 * klen + GROUP
    depth = round_up(owners // 2 * 3 * TILE, LANES)
    blocks = SEGLEN // LANES
    in_vmem = pl.BlockSpec(memory_space=pltpu.VMEM)
    in_smem = pl.BlockSpec(memory_space=pltpu.SMEM)
    in_hbm = pl.BlockSpec(memory_space=pltpu.HBM)
    ordered, table, coupling, plan = pl.pallas_call(
        functools.partial(gather_kernel, owners, shards),
        out_shape=(
            pltpu.VMEM(((samples + klen) // LANES + 1, height, LANES), jnp.float32),
            pltpu.VMEM((klen + LANES, filters * LANES), jnp.bfloat16),
            pltpu.VMEM((crystals, slot, LANES), jnp.float32),
            pltpu.VMEM((2, LANES), jnp.int32),
        ),
        in_specs=[in_hbm] * 4 + [in_smem] * 2,
        out_specs=(in_vmem,) * 4,
        scratch_shapes=[
            pltpu.VMEM((2, rows, klen), jnp.bfloat16),
            pltpu.VMEM(kernels.shape, kernels.dtype),
            pltpu.VMEM(chan_map.shape, chan_map.dtype),
            pltpu.VMEM((sig, crystals, sig), crosstalk.dtype),
            pltpu.VMEM((2, owners, TILE, packed), jnp.bfloat16),
            pltpu.VMEM((3, owners, TILE, packed), jnp.bfloat16),
            pltpu.VMEM((2, TILE // (sig - 2 * TILE), height, depth), jnp.bfloat16),
            pltpu.VMEM((2 * depth, LANES), jnp.float32),
            pltpu.VMEM((height, LANES), jnp.float32),
            pltpu.SemaphoreType.DMA((2,)),
            pltpu.SemaphoreType.DMA((3,)),
            pltpu.SemaphoreType.DMA((2, owners)),
            pltpu.SemaphoreType.DMA((2, owners)),
            pltpu.SemaphoreType.DMA((owners,)),
            pltpu.SemaphoreType.DMA((owners,)),
        ],
        compiler_params=pltpu.CompilerParams(
            collective_id=0, has_side_effects=True, vmem_limit_bytes=VMEM_BYTES
        ),
        name="gather_rows",
    )(
        signals,
        kernels,
        chan_map,
        jnp.transpose(crosstalk, (1, 0, 2)),
        starts.reshape(-1),
        counts.reshape(-1),
    )
    built = pl.pallas_call(
        functools.partial(build_kernel, sig),
        out_shape=jax.ShapeDtypeStruct((crystals, sig * blocks * filters, LANES), jnp.bfloat16),
        in_specs=[in_vmem] * 3 + [in_smem],
        out_specs=in_hbm,
        scratch_shapes=[
            pltpu.VMEM((crystals, slot * blocks * filters, LANES), jnp.float32),
            pltpu.VMEM((crystals, sig * blocks * filters, LANES), jnp.bfloat16),
            pltpu.SemaphoreType.DMA((crystals,)),
        ],
        compiler_params=pltpu.CompilerParams(vmem_limit_bytes=24 * 1024 * 1024),
        name="build_events",
    )(ordered, table, coupling, plan)
    parts = built.reshape(crystals, sig, blocks, filters, LANES)
    return jnp.transpose(parts, (0, 3, 1, 2, 4)).reshape(crystals, 1, slots, filters, sig, SEGLEN)


def solution(mesh):
    return jax.shard_map(
        body,
        mesh=mesh,
        in_specs=(
            P("chan", "tm"),
            P(),
            P(),
            P("chan", None, None),
            P(None, "tm", None),
            P(None, "tm"),
        ),
        out_specs=P("chan", "tm", None, None, None, None),
        check_vma=False,
    )
```

```python
import functools

import jax
import jax.numpy as jnp
from jax import lax
from jax.experimental import pallas as pl
from jax.experimental.pallas import tpu as pltpu
from jax.sharding import PartitionSpec as P

SEGLEN = 512
PRE = 128
LANES = 128
TILE = 16
GROUP = 256
SLOT_ROWS = 8
VMEM_BYTES = 56 * 1024 * 1024
MESH = pl.DeviceIdType.MESH


def round_up(value, step):
    return -(-value // step) * step


def iota(shape, axis):
    return lax.broadcasted_iota(jnp.int32, shape, axis)


def gather_kernel(
    owners, shards, x_ref, taps_hbm, map_hbm, cross_hbm, starts_ref, counts_ref,
    ordered, table, coupling, plan,
    held, taps_ref, map_ref, cross_ref, pack, arrived, placer, slots_ref, cross,
    load_sem, small_sem, chan_send, chan_recv, tail_send, tail_recv,
):
    me = lax.axis_index("chan")
    shard = lax.axis_index("tm")
    rows, samples = x_ref.shape
    klen = taps_ref.shape[1]
    sig, crystals = cross_ref.shape[0], cross_ref.shape[1]
    main = 2 * TILE
    rest = sig - main
    groups = TILE // rest
    slot = round_up(sig, SLOT_ROWS)
    height = crystals * slot
    blocks = (samples + klen) // LANES
    half_blocks = klen // LANES
    later = shard < shards - 1

    def load(half):
        return pltpu.make_async_copy(
            x_ref.at[:, half * klen : (half + 1) * klen], held.at[half], load_sem.at[half]
        )

    small = [
        pltpu.make_async_copy(source, target, small_sem.at[at])
        for at, (source, target) in enumerate(
            [(taps_hbm, taps_ref), (map_hbm, map_ref), (cross_hbm, cross_ref)]
        )
    ]
    load(1).start()
    load(0).start()
    for copy in small:
        copy.start()

    def partner(step):
        if owners & (owners - 1) == 0:
            return me ^ step, me ^ step
        return lax.rem(me + step, owners), lax.rem(me + owners - step, owners)

    steps = sorted(range(2, owners), key=lambda step: (-bin(step >> 1).count("1"), step & 1, step))
    steps = [1] + steps if owners > 1 else []
    place_of = {step: at for at, step in enumerate([0] + steps)}
    splits = 2
    share = owners // splits
    span = share * (main + TILE)
    depth = round_up(span, LANES)

    barrier = pltpu.get_barrier_semaphore()
    for step in range(1, owners):
        pl.semaphore_signal(
            barrier, inc=1, device_id={"chan": partner(step)[0]}, device_id_type=MESH
        )

    @pl.when(shard > 0)
    def _():
        pl.semaphore_signal(barrier, inc=1, device_id={"tm": shard - 1}, device_id_type=MESH)

    def rest_row(index):
        turned = index - main
        for group in range(1, groups):
            turned = turned - jnp.where(index >= main + group * rest, rest, 0)
        return jnp.where(index < main, index, main + turned)

    def pack_half(half):
        load(half).wait()
        for owner in range(owners):
            base = owner * sig
            low = base // TILE * TILE
            high = min(round_up(base + sig, TILE), rows)
            shape = (main + TILE, high - low)
            index = iota(shape, 0)
            wanted = base + rest_row(index)
            hit = jnp.logical_and(iota(shape, 1) + low == wanted, index < main + groups * rest)
            picker = jnp.where(hit, 1.0, 0.0).astype(jnp.bfloat16)
            picked = jnp.dot(picker, held[half, low:high, :], preferred_element_type=jnp.float32)
            pack[half, owner, :, 0:klen] = picked[0:TILE].astype(jnp.bfloat16)
            pack[half, owner, :, klen : 2 * klen] = picked[TILE:main].astype(jnp.bfloat16)
            left = picked[main:]
            last = left[:, 2 * GROUP : klen]
            row = iota((TILE, GROUP), 0)
            kept = jnp.where(
                row < rest,
                left[:, 0:GROUP],
                jnp.where(row < 2 * rest, left[:, GROUP : 2 * GROUP], jnp.concatenate([last, last], axis=1)),
            )
            pack[half, owner, :, 2 * klen : 2 * klen + GROUP] = kept.astype(jnp.bfloat16)
        arrived[half + 1, 0] = pack[half, me]

    pack_half(1)

    @pl.when(shard == 0)
    def _():
        arrived[0] = jnp.zeros(arrived.shape[1:], arrived.dtype)

    pl.semaphore_wait(barrier, owners - 1 + jnp.where(later, 1, 0))

    def to_owner(half, step):
        peer = partner(step)[0]
        return pltpu.make_async_remote_copy(
            src_ref=pack.at[half, peer],
            dst_ref=arrived.at[half + 1, place_of[step]],
            send_sem=chan_send.at[half, step],
            recv_sem=chan_recv.at[half, step],
            device_id={"chan": peer},
            device_id_type=MESH,
        )

    def from_owner(half, step):
        peer = partner(step)[1]
        return pltpu.make_async_remote_copy(
            src_ref=pack.at[half, peer],
            dst_ref=arrived.at[half + 1, place_of[step]],
            send_sem=chan_send.at[half, step],
            recv_sem=chan_recv.at[half, step],
            device_id={"chan": peer},
            device_id_type=MESH,
        )

    def onward(step):
        return pltpu.make_async_remote_copy(
            src_ref=arrived.at[2, place_of[step]],
            dst_ref=arrived.at[0, place_of[step]],
            send_sem=tail_send.at[step],
            recv_sem=tail_recv.at[step],
            device_id={"tm": jnp.minimum(shard + 1, shards - 1)},
            device_id_type=MESH,
        )

    for step in steps:
        to_owner(1, step).start()

    @pl.when(later)
    def _():
        onward(0).start()

    pack_half(0)
    for step in steps:
        to_owner(0, step).start()

    for copy in small:
        copy.wait()

    taps = taps_ref[...].astype(jnp.float32)
    square = (LANES, LANES)
    upper = iota(square, 1) >= iota(square, 0)
    nothing = jnp.zeros(square, jnp.float32)
    for filter_index in range(taps.shape[0]):
        turned = []
        for block in range(half_blocks):
            row = taps[filter_index : filter_index + 1, block * LANES : (block + 1) * LANES]
            turned.append(pltpu.roll(jnp.broadcast_to(row, square), 0, 1, stride=1, stride_axis=0))
        turned.append(nothing)
        for block in range(half_blocks + 1):
            above = turned[half_blocks - block]
            below = turned[half_blocks - 1 - block] if block < half_blocks else nothing
            table[
                block * LANES : (block + 1) * LANES,
                filter_index * LANES : (filter_index + 1) * LANES,
            ] = jnp.where(upper, above, below).astype(table.dtype)

    for step in steps:
        from_owner(1, step).wait_recv()

        @pl.when(later)
        def _():
            onward(step).start()

    slots_ref[...] = jnp.full(slots_ref.shape, -5.0, slots_ref.dtype)
    total = map_ref.shape[0]
    for source in range(owners):
        low = source * rows // LANES * LANES
        high = min(round_up((source + 1) * rows, LANES), total)
        shape = (main + TILE, high - low)
        index = iota(shape, 0)
        wanted = source * rows + me * sig + rest_row(index)
        hit = jnp.logical_and(iota(shape, 1) + low == wanted, index < main + groups * rest)
        names = (map_ref[low:high].astype(jnp.float32) + 1.0).reshape(1, high - low)
        column = jnp.sum(jnp.where(hit, names, 0.0), axis=1, keepdims=True)
        column = jnp.broadcast_to(column, (main + TILE, LANES))
        step_to = me ^ source if owners & (owners - 1) == 0 else lax.rem(me - source + owners, owners)
        at = 0
        for step, place_at in place_of.items():
            first = place_at // share * depth + place_at % share * TILE
            at = at + jnp.where(step_to == step, first, 0)
        for part in range(3):
            target = pl.ds(pl.multiple_of(at + part * share * TILE, TILE), TILE)
            slots_ref[target, :] = column[part * TILE : (part + 1) * TILE]
    column = slots_ref[:, 0:1]
    width = round_up(height, LANES)
    lane = iota((1, width), 1)
    crystal_of = jnp.zeros((1, width), jnp.int32)
    for crystal in range(1, crystals):
        crystal_of = crystal_of + jnp.where(lane >= crystal * slot, 1, 0)
    signal_of = lane - crystal_of * slot
    wanted = jnp.where(signal_of < sig, crystal_of * sig + signal_of + me * rows + 1, -1)
    matched = jnp.where(column == wanted.astype(jnp.float32), 1.0, 0.0)
    turned = jnp.transpose(matched)[0:height]
    lane = iota((1, LANES), 1)
    begins = jnp.zeros((1, LANES), jnp.int32)
    lives = jnp.zeros((1, LANES), jnp.int32)
    for crystal in range(crystals):
        begins = jnp.where(lane == crystal, starts_ref[me * crystals + crystal], begins)
        lives = jnp.where(lane == crystal, counts_ref[me * crystals + crystal], lives)
    plan[0:1] = begins
    plan[1:2] = lives

    cross[...] = jnp.zeros(cross.shape, cross.dtype)
    cross[0 : sig * crystals, 0:sig] = cross_ref[...].astype(jnp.float32).reshape(sig * crystals, sig)
    for crystal in range(crystals):
        coupling[crystal] = cross[pl.ds(crystal, slot, stride=crystals), :]
    lane = iota((height, depth), 1)
    part_of = jnp.where(lane < share * main, -1, lane & (TILE - 1))
    for group in range(groups):
        own = jnp.logical_and(part_of >= group * rest, part_of < (group + 1) * rest)
        keep = jnp.logical_or(part_of < 0, own)
        for split in range(splits):
            own = turned[:, split * depth : (split + 1) * depth]
            placer[split, group] = jnp.where(keep, own, 0.0).astype(placer.dtype)

    def place(part, first_block, split):
        source = arrived[part, split * share : (split + 1) * share]
        source = source.reshape(share * TILE, arrived.shape[3])
        for group in range(groups):
            low = group * GROUP
            high = min(low + GROUP, klen)
            stacked = jnp.concatenate(
                [
                    source[:, low:high],
                    source[:, klen + low : klen + high],
                    source[:, 2 * klen : 2 * klen + high - low],
                ],
                axis=0,
            )
            rows_out = jnp.dot(
                placer[split, group][:, 0:span], stacked, preferred_element_type=jnp.float32)
            for block in range((high - low) // LANES):
                at = first_block + low // LANES + block
                piece = rows_out[:, block * LANES : (block + 1) * LANES]
                ordered[at] = piece if split == 0 else ordered[at] + piece

    members = [[step for step in place_of if place_of[step] // share == split] for split in range(splits)]
    for split in range(splits):
        place(2, 2 * half_blocks, split)
    for split in range(splits):
        for step in members[split]:
            if step:
                from_owner(0, step).wait_recv()
        place(1, half_blocks, split)

        @pl.when(shard > 0)
        def _():
            for step in members[split]:
                onward(step).wait_recv()

        place(0, 0, split)
    ordered[blocks] = jnp.zeros(ordered.shape[1:], ordered.dtype)

    for step in steps:
        to_owner(1, step).wait_send()
        to_owner(0, step).wait_send()

    @pl.when(later)
    def _():
        for step in range(owners):
            onward(step).wait_send()


def build_kernel(
    sig, ordered, table, coupling, plan, out_ref, rows_of, built, out_sem
):
    crystals, slot = coupling.shape[0], coupling.shape[1]
    filters = table.shape[1] // LANES
    half_blocks = table.shape[0] // LANES - 1
    klen = half_blocks * LANES

    window_blocks = (SEGLEN + klen) // LANES
    seg_blocks = SEGLEN // LANES
    steps_back = half_blocks + 1
    lane = iota((slot, LANES), 1)
    center = (PRE - 1) / 2.0
    fit_axis = [
        (iota((1, LANES), 1).astype(jnp.float32) + (block * LANES - center)) / (PRE / 2.0)
        for block in range(seg_blocks)
    ]
    pre_axis = fit_axis[0]
    power = jnp.sum(pre_axis * pre_axis)
    taps_table = table[...]
    pair = 2 if crystals % 2 == 0 else 1
    high = pair * slot
    for crystal in range(0, crystals, pair):
        windows = []
        for member in range(crystal, crystal + pair):
            start = plan[0, member]
            first = start >> 7
            shift = start & (LANES - 1)
            back = (LANES - shift) & (LANES - 1)
            at = slice(member * slot, (member + 1) * slot)
            rolled = [
                pltpu.roll(ordered[first + block, at, :], back, 1)
                for block in range(window_blocks + 1)
            ]
            windows.append(
                [
                    jnp.where(lane < LANES - shift, rolled[block], rolled[block + 1])
                    for block in range(window_blocks)
                ]
            )
        cut = [
            jnp.concatenate([w[block] for w in windows], axis=0).astype(jnp.bfloat16)
            for block in range(window_blocks)
        ]
        wide = jnp.concatenate(
            [jnp.concatenate(cut[b : b + steps_back], axis=1) for b in range(seg_blocks)], axis=0
        )
        filtered = jnp.dot(wide, taps_table, preferred_element_type=jnp.float32)
        for member in range(pair):
            at = crystal + member
            live = plan[1, at] > 0
            pieces = jnp.concatenate(
                [
                    filtered[b * high + member * slot : b * high + (member + 1) * slot]
                    for b in range(seg_blocks)
                ],
                axis=1,
            ).astype(jnp.bfloat16)
            mixer = coupling[at][:, 0:slot].astype(jnp.bfloat16)
            coupled = pieces.astype(jnp.float32) + jnp.dot(
                mixer, pieces, preferred_element_type=jnp.float32
            )
            for filter_index in range(filters):
                own = [
                    coupled[:, (b * filters + filter_index) * LANES :][:, :LANES]
                    for b in range(seg_blocks)
                ]
                offset_fit = jnp.mean(own[0], axis=1, keepdims=True)
                slope_fit = jnp.sum(own[0] * pre_axis, axis=1, keepdims=True) / power
                for b in range(seg_blocks):
                    fitted = own[b] - offset_fit - slope_fit * fit_axis[b]
                    rows_of[
                        at, pl.ds(b * filters + filter_index, slot, stride=filters * seg_blocks), :
                    ] = jnp.where(live, fitted, 0.0)
        for at in range(crystal, crystal + pair):
            built[at] = rows_of[at, 0 : built.shape[1], :].astype(built.dtype)
        for at in range(crystal, crystal + pair):
            pltpu.make_async_copy(built.at[at], out_ref.at[at], out_sem.at[at]).start()
    for at in range(crystals):
        pltpu.make_async_copy(built.at[at], out_ref.at[at], out_sem.at[at]).wait()


def body(signals, kernels, chan_map, crosstalk, starts, counts):
    owners = lax.axis_size("chan")
    shards = lax.axis_size("tm")
    rows, samples = signals.shape
    filters, klen = kernels.shape
    crystals, sig, _ = crosstalk.shape
    slots = starts.shape[2]
    slot = round_up(sig, SLOT_ROWS)
    height = crystals * slot
    packed = 2 * klen + GROUP
    depth = round_up(owners // 2 * 3 * TILE, LANES)
    blocks = SEGLEN // LANES
    in_vmem = pl.BlockSpec(memory_space=pltpu.VMEM)
    in_smem = pl.BlockSpec(memory_space=pltpu.SMEM)
    in_hbm = pl.BlockSpec(memory_space=pltpu.HBM)
    ordered, table, coupling, plan = pl.pallas_call(
        functools.partial(gather_kernel, owners, shards),
        out_shape=(
            pltpu.VMEM(((samples + klen) // LANES + 1, height, LANES), jnp.float32),
            pltpu.VMEM((klen + LANES, filters * LANES), jnp.bfloat16),
            pltpu.VMEM((crystals, slot, LANES), jnp.float32),
            pltpu.VMEM((2, LANES), jnp.int32),
        ),
        in_specs=[in_hbm] * 4 + [in_smem] * 2,
        out_specs=(in_vmem,) * 4,
        scratch_shapes=[
            pltpu.VMEM((2, rows, klen), jnp.bfloat16),
            pltpu.VMEM(kernels.shape, kernels.dtype),
            pltpu.VMEM(chan_map.shape, chan_map.dtype),
            pltpu.VMEM((sig, crystals, sig), crosstalk.dtype),
            pltpu.VMEM((2, owners, TILE, packed), jnp.bfloat16),
            pltpu.VMEM((3, owners, TILE, packed), jnp.bfloat16),
            pltpu.VMEM((2, TILE // (sig - 2 * TILE), height, depth), jnp.bfloat16),
            pltpu.VMEM((2 * depth, LANES), jnp.float32),
            pltpu.VMEM((height, LANES), jnp.float32),
            pltpu.SemaphoreType.DMA((2,)),
            pltpu.SemaphoreType.DMA((3,)),
            pltpu.SemaphoreType.DMA((2, owners)),
            pltpu.SemaphoreType.DMA((2, owners)),
            pltpu.SemaphoreType.DMA((owners,)),
            pltpu.SemaphoreType.DMA((owners,)),
        ],
        compiler_params=pltpu.CompilerParams(
            collective_id=0, has_side_effects=True, vmem_limit_bytes=VMEM_BYTES
        ),
        name="gather_rows",
    )(
        signals,
        kernels,
        chan_map,
        jnp.transpose(crosstalk, (1, 0, 2)),
        starts.reshape(-1),
        counts.reshape(-1),
    )
    built = pl.pallas_call(
        functools.partial(build_kernel, sig),
        out_shape=jax.ShapeDtypeStruct((crystals, sig * blocks * filters, LANES), jnp.bfloat16),
        in_specs=[in_vmem] * 3 + [in_smem],
        out_specs=in_hbm,
        scratch_shapes=[
            pltpu.VMEM((crystals, slot * blocks * filters, LANES), jnp.float32),
            pltpu.VMEM((crystals, sig * blocks * filters, LANES), jnp.bfloat16),
            pltpu.SemaphoreType.DMA((crystals,)),
        ],
        compiler_params=pltpu.CompilerParams(vmem_limit_bytes=24 * 1024 * 1024),
        name="build_events",
    )(ordered, table, coupling, plan)
    parts = built.reshape(crystals, sig, blocks, filters, LANES)
    return jnp.transpose(parts, (0, 3, 1, 2, 4)).reshape(crystals, 1, slots, filters, sig, SEGLEN)


def solution(mesh):
    return jax.shard_map(
        body,
        mesh=mesh,
        in_specs=(
            P("chan", "tm"),
            P(),
            P(),
            P("chan", None, None),
            P(None, "tm", None),
            P(None, "tm"),
        ),
        out_specs=P("chan", "tm", None, None, None, None),
        check_vma=False,
    )
```
